512 devices in a mesh: vocab: 32 (over x, y, core), dp: 16 (over z).
Axes of the slice: x: 4, y: 4, z: 16, core: 2. Of those that a mesh axis runs over, the one named last changes fastest.
Arguments:
- hidden: bfloat16 [2048, 2048], P('dp', 'vocab')
- head_weight: bfloat16 [2048, 65536], P('dp', 'vocab')
- teacher_logits: bfloat16 [2048, 65536], P('dp', 'vocab')
- target_ids: int32 [2048], P('dp'), may hold values from 0 to 65535
- segment_ids: int32 [16, 128], P('dp'), may hold values from 0 to 15, never falling along the last dimension, each value on 1 to 16 neighbouring positions
- pair_order: int32 [16, 16], P('dp'), may hold values from 0 to 15, each once within a row
Outputs:
- hidden_grad: bfloat16 [2048, 2048], P('dp', 'vocab')
- head_grad: float32 [2048, 65536], P('dp', 'vocab')
- loss: float32 [], replicated
The draws below stay inside these ranges and needn't reach their ends.
Inputs may be any that keep to these rules, and one draw needn't show every extreme that they name: `segment_ids`: in each group the row's sequence number never falls along the rows, and every sequence has 1 to 16 rows. `pair_order`: each group's row is a permutation of its 16 sequences; pair p is entry 2p (chosen) and entry 2p + 1 (rejected).
All inputs are finite; a program needn't handle non-finite values.
Results may differ from the reference program's by a relative error of at most 0.018.
Values may be sent and summed in bfloat16 or wider, within the bound.
No kernel may reach another device: no remote copies, remote signals or barrier semaphores. Data moves between devices by JAX's collectives and lax.ppermute only.
A program may use at most 64 MiB of HBM per device.

```python
import math
import jax
import jax.numpy as jnp
import numpy as np
from jax import lax

D = 2048
V_DEV = 2048
R = 128
SEQS = 16
MOST = 16
GROUPS = 16
ROWS = 2048
VOCAB = 65536
N_VOCAB = 32


def group_factor(low, high):
    group_number = (jnp.arange(ROWS, dtype=jnp.int32) // R).astype(jnp.float32)
    fraction = group_number / max(GROUPS - 1, 1)
    return (low * jnp.exp(fraction * math.log(high / low)))[:, None]


def draw_hidden(key, part):
    own_key = jax.random.fold_in(key, 11)
    key_noise = jax.random.fold_in(own_key, 0)
    key_scale = jax.random.fold_in(own_key, 1)
    key_common = jax.random.fold_in(own_key, 4)
    key_share = jax.random.fold_in(own_key, 5)
    row_scale = jnp.exp(jax.random.uniform(key_scale, (ROWS, 1), jnp.float32, math.log(0.5), math.log(2.0)))
    common = jnp.clip(jax.random.normal(key_common, (1, D), jnp.float32), -3.0, 3.0)
    share = jax.random.uniform(key_share, (ROWS, 1), jnp.float32, 0.5, 1.5)
    noise = jnp.clip(jax.random.normal(key_noise, (ROWS, D), jnp.float32), -5.0, 5.0)
    values = (noise * row_scale + 0.7 * share * common) * group_factor(0.5, 2.0) / 3.0
    return values.astype(jnp.bfloat16)


def draw_head_weight(key, part):
    own_key = jax.random.fold_in(key, 13)
    values = jnp.clip(jax.random.normal(own_key, (D, VOCAB), jnp.float32), -6.0, 6.0) * (3.0 / math.sqrt(D))
    return values.astype(jnp.bfloat16)


def draw_teacher_logits(key, part):
    own_key = jax.random.fold_in(key, 17)
    keys = jax.random.split(own_key, 11)
    col_scale = jnp.exp(jax.random.uniform(keys[1], (1, VOCAB), jnp.float32, math.log(0.5), math.log(2.0)))
    row_numbers = jnp.arange(ROWS)
    spiked = jax.random.randint(keys[8], (ROWS,), 0, 4) != 0
    height = jax.random.uniform(keys[9], (ROWS,), jnp.float32, 8.0, 10.0)
    spike_col = jax.random.randint(keys[10], (ROWS,), 0, VOCAB)
    offset = 0.7 * jnp.clip(jax.random.normal(keys[7], (1, VOCAB), jnp.float32), -4.0, 4.0)
    values = jnp.clip(jax.random.normal(keys[0], (ROWS, VOCAB), jnp.float32), -6.0, 6.0) * col_scale + offset
    values = values.at[row_numbers, spike_col].add(jnp.where(spiked, height, 0.0))
    return values.astype(jnp.bfloat16)


def set_ends(values, rng, smallest, largest):
    dims = values.shape
    place = [jax.random.randint(jax.random.fold_in(rng, axis), (), 0, dims[axis]) for axis in range(len(dims))]
    values = values.at[tuple(place)].set(smallest)
    longest = dims.index(max(dims))
    place[longest] = (place[longest] + 1) % dims[longest]
    return values.at[tuple(place)].set(largest)


def cumulative_ranks(number_of, slope):
    weights = [(1 << 20) // math.isqrt(rank ** slope) + 1 for rank in range(1, number_of + 1)]
    width = 1 + sum(weights) // (1 << 30)
    return np.cumsum(np.array([max(1, weight // width) for weight in weights]))


def ranked(rng, extent, number_of, lean):
    grid = cumulative_ranks(number_of, lean)
    ticket = jax.random.randint(jax.random.fold_in(rng, 1), extent, 0, int(grid[number_of - 1]))
    grade = jnp.searchsorted(jnp.asarray(grid, jnp.int32), ticket, side="right")
    return jax.random.permutation(jax.random.fold_in(rng, 2), number_of)[grade].astype(jnp.int32)


def length_profile(number_of, total, most, slope):
    loads = [(1 << 20) // math.isqrt(rank ** slope) + 1 for rank in range(2, number_of + 1)]
    surplus, given = total - most - (number_of - 1), [1] * (number_of - 1)
    while surplus > 0:
        candidates = [i for i in range(number_of - 1) if given[i] < most]
        mass, remaining = sum([loads[i] for i in candidates]), surplus
        for i in candidates:
            extra = min(most - given[i], max(1, remaining * loads[i] // mass), surplus)
            given[i] = given[i] + extra
            surplus = surplus - extra
    return np.array([most] + given)


def uneven_parts(key, number_of, total, most, slope):
    if number_of == 2:
        one = jax.random.randint(key, (), max(1, total - most), min(most, total - 1) + 1)
        return jnp.stack([one, total - one])
    sizes = jnp.asarray(length_profile(number_of, total, most, slope), jnp.int32)
    twos = (number_of - 1) // 2
    donor, taker = sizes[1:1 + 2 * twos:2], sizes[2:2 + 2 * twos:2]
    room = jnp.minimum(donor - 1, most - taker)
    passed = jax.random.randint(jax.random.fold_in(key, 1), (twos,), 0, 1 << 20) % (room + 1)
    sizes = sizes.at[1:1 + 2 * twos:2].set(donor - passed).at[2:2 + 2 * twos:2].set(taker + passed)
    return sizes[jax.random.permutation(jax.random.fold_in(key, 2), number_of)]


def setup_inputs(seed: int = 0) -> dict:
    seeds = jax.random.split(jax.random.key(seed), 7)
    return {
        "hidden": draw_hidden(jax.random.fold_in(seeds[6], 71), 0),
        "head_weight": draw_head_weight(jax.random.fold_in(seeds[6], 71), 0),
        "teacher_logits": draw_teacher_logits(jax.random.fold_in(seeds[6], 71), 0),
        "target_ids": set_ends(ranked(seeds[3], (ROWS,), VOCAB, 2), jax.random.fold_in(seeds[3], 3), 0, VOCAB - 1).astype(jnp.int32),
        "segment_ids": jax.vmap(lambda own: jnp.searchsorted(jnp.cumsum(uneven_parts(own, SEQS, R, MOST, 1)), jnp.arange(R), side="right"))(jax.random.split(seeds[4], GROUPS)).reshape((GROUPS, R)).astype(jnp.int32),
        "pair_order": jax.vmap(lambda own: jax.random.permutation(own, SEQS))(jax.random.split(seeds[5], GROUPS)).reshape((GROUPS, SEQS)).astype(jnp.int32),
    }


dpo_beta = 0.1
dpo_gamma = 4.0


def pair_weights(log_ratio, segments, ordering):
    seq_count = ordering.shape[0]
    labels = lax.broadcasted_iota(jnp.int32, (1, seq_count), 1)
    seq_hot = (segments[:, None] == labels).astype(jnp.float32)
    seq_ratio = jnp.sum(seq_hot * log_ratio[:, None], axis=0)
    chosen = ordering[0::2]
    rejected = ordering[1::2]
    chosen_hot = (chosen[:, None] == labels).astype(jnp.float32)
    rejected_hot = (rejected[:, None] == labels).astype(jnp.float32)
    margin = dpo_beta * (jnp.sum(chosen_hot * seq_ratio[None, :], axis=1) - jnp.sum(rejected_hot * seq_ratio[None, :], axis=1))
    strength = dpo_gamma * dpo_beta * jax.nn.sigmoid(-margin)
    coeffs = jnp.sum((rejected_hot - chosen_hot) * strength[:, None], axis=0)
    row_weight = jnp.sum(seq_hot * coeffs[None, :], axis=1)
    return row_weight, jnp.sum(jax.nn.softplus(-margin))


def group_terms(student, teacher, targets, segments, ordering):
    max_student = jnp.max(student, axis=1)
    exp_student = jnp.exp(student - max_student[:, None])
    sum_student = jnp.sum(exp_student, axis=1)
    max_teacher = jnp.max(teacher, axis=1)
    exp_teacher = jnp.exp(teacher - max_teacher[:, None])
    sum_teacher = jnp.sum(exp_teacher, axis=1)
    cross = jnp.sum(exp_teacher * (teacher - student), axis=1)
    lse_student = max_student + jnp.log(sum_student)
    lse_teacher = max_teacher + jnp.log(sum_teacher)
    kl_rows = cross / sum_teacher - lse_teacher + lse_student
    is_target = lax.broadcasted_iota(jnp.int32, student.shape, 1) == targets[:, None]
    target_student = jnp.sum(jnp.where(is_target, student, 0.0), axis=1)
    target_teacher = jnp.sum(jnp.where(is_target, teacher, 0.0), axis=1)
    log_ratio = (target_student - lse_student) - (target_teacher - lse_teacher)
    row_weight, dpo_sum = pair_weights(log_ratio, segments, ordering)
    prob_student = exp_student / sum_student[:, None]
    prob_teacher = exp_teacher / sum_teacher[:, None]
    logit_grad = prob_student - prob_teacher + row_weight[:, None] * (is_target.astype(jnp.float32) - prob_student)
    return logit_grad.astype(jnp.bfloat16), jnp.sum(kl_rows) + dpo_gamma * dpo_sum


def reference(hidden, head_weight, teacher_logits, target_ids, segment_ids, pair_order):
    def one_group(inputs):
        group_rows, group_teacher, group_targets, segments, ordering = inputs
        student = jnp.dot(group_rows, head_weight, preferred_element_type=jnp.float32)
        return group_terms(student, group_teacher.astype(jnp.float32), group_targets, segments, ordering)

    group_grads, objectives = lax.map(one_group, (hidden.reshape(GROUPS, R, D), teacher_logits.reshape(GROUPS, R, VOCAB), target_ids.reshape(GROUPS, R), segment_ids, pair_order))
    loss_value = jnp.sum(objectives) / ROWS
    logit_grad = group_grads.reshape(ROWS, VOCAB)
    head_grad = jnp.dot(hidden.T, logit_grad, preferred_element_type=jnp.float32)

    def add_shard(running, shard_index):
        first_col = (shard_index * V_DEV).astype(jnp.int32)
        grad_shard = lax.dynamic_slice_in_dim(logit_grad, first_col, V_DEV, 1)
        weight_shard = lax.dynamic_slice_in_dim(head_weight, first_col, V_DEV, 1)
        partial_value = lax.dot_general(grad_shard, weight_shard, (((1,), (1,)), ((), ())), preferred_element_type=jnp.float32)
        rounded = lax.optimization_barrier(partial_value.astype(jnp.bfloat16))
        return running + rounded.astype(jnp.float32), None

    summed, _ = lax.scan(add_shard, jnp.zeros((ROWS, D), jnp.float32), jnp.arange(N_VOCAB, dtype=jnp.int32))
    return summed.astype(jnp.bfloat16), head_grad, loss_value
```

```python
import jax
import jax.numpy as jnp
from jax import lax
from jax.sharding import PartitionSpec as P

dpo_beta = 0.1
dpo_gamma = 4.0


def pair_weights(log_ratio, segments, ordering):
    seq_count = ordering.shape[0]
    labels = lax.broadcasted_iota(jnp.int32, (1, seq_count), 1)
    seq_hot = (segments[:, None] == labels).astype(jnp.float32)
    seq_ratio = jnp.sum(seq_hot * log_ratio[:, None], axis=0)
    chosen = ordering[0::2]
    rejected = ordering[1::2]
    chosen_hot = (chosen[:, None] == labels).astype(jnp.float32)
    rejected_hot = (rejected[:, None] == labels).astype(jnp.float32)
    margin = dpo_beta * (
        jnp.sum(chosen_hot * seq_ratio[None, :], axis=1)
        - jnp.sum(rejected_hot * seq_ratio[None, :], axis=1)
    )
    strength = dpo_gamma * dpo_beta * jax.nn.sigmoid(-margin)
    coeffs = jnp.sum((rejected_hot - chosen_hot) * strength[:, None], axis=0)
    row_weight = jnp.sum(seq_hot * coeffs[None, :], axis=1)
    return (row_weight, jnp.sum(jax.nn.softplus(-margin)))


def to_all(block, axis):
    count = lax.axis_size(axis)
    copies = jnp.broadcast_to(block[None], (count,) + block.shape)
    return lax.all_to_all(copies, axis, 0, 0, tiled=True)


def on_device(hidden, head_weight, teacher_logits, target_ids, segment_ids, pair_order):
    f32, bf16 = jnp.float32, jnp.bfloat16
    rows_full = lax.all_gather(hidden, "vocab", axis=1, tiled=True)
    width = head_weight.shape[1]
    half = width // 2
    weight_lo = lax.all_gather(head_weight[:, :half], "dp", axis=0, tiled=True)
    weight_hi = lax.all_gather(head_weight[:, half:], "dp", axis=0, tiled=True)
    student = jnp.concatenate(
        [
            jnp.dot(rows_full, weight_lo, preferred_element_type=f32),
            jnp.dot(rows_full, weight_hi, preferred_element_type=f32),
        ],
        axis=1,
    )
    teacher = teacher_logits.astype(f32)
    n_vocab = lax.axis_size("vocab")
    n_dp = lax.axis_size("dp")
    rows = student.shape[0]
    offset = lax.axis_index("vocab") * width
    column = lax.broadcasted_iota(jnp.int32, student.shape, 1) + offset
    is_target = column == target_ids[:, None]
    own_max = jnp.max(student, axis=1)
    own_tmax = jnp.max(teacher, axis=1)
    own_exp = jnp.exp(student - own_max[:, None])
    own_texp = jnp.exp(teacher - own_tmax[:, None])
    stats = jnp.stack(
        [
            own_max,
            own_tmax,
            jnp.sum(own_exp, axis=1),
            jnp.sum(own_texp, axis=1),
            jnp.sum(own_texp * (teacher - student), axis=1),
            jnp.sum(jnp.where(is_target, student, 0.0), axis=1),
            jnp.sum(jnp.where(is_target, teacher, 0.0), axis=1),
            jnp.zeros((rows,), f32),
        ]
    )
    every = to_all(stats, "vocab").reshape(n_vocab, 8, rows)
    max_student = jnp.max(every[:, 0], axis=0)
    max_teacher = jnp.max(every[:, 1], axis=0)
    scale_s = jnp.exp(every[:, 0] - max_student[None])
    scale_t = jnp.exp(every[:, 1] - max_teacher[None])
    sum_student = jnp.sum(every[:, 2] * scale_s, axis=0)
    sum_teacher = jnp.sum(every[:, 3] * scale_t, axis=0)
    cross = jnp.sum(every[:, 4] * scale_t, axis=0)
    target_student = jnp.sum(every[:, 5], axis=0)
    target_teacher = jnp.sum(every[:, 6], axis=0)
    lse_student = max_student + jnp.log(sum_student)
    lse_teacher = max_teacher + jnp.log(sum_teacher)
    kl_rows = cross / sum_teacher - lse_teacher + lse_student
    log_ratio = target_student - lse_student - (target_teacher - lse_teacher)
    row_weight, dpo_sum = pair_weights(log_ratio, segment_ids[0], pair_order[0])
    group_objective = jnp.sum(kl_rows) + dpo_gamma * dpo_sum
    exp_student = jnp.exp(student - max_student[:, None])
    exp_teacher = jnp.exp(teacher - max_teacher[:, None])
    prob_student = exp_student / sum_student[:, None]
    prob_teacher = exp_teacher / sum_teacher[:, None]
    logit_grad = (
        prob_student
        - prob_teacher
        + row_weight[:, None] * (is_target.astype(f32) - prob_student)
    ).astype(bf16)
    grad_lo = logit_grad[:, :half]
    grad_hi = logit_grad[:, half:]
    all_lo = lax.all_gather(grad_lo, "dp", axis=0, tiled=True)
    all_hi = lax.all_gather(grad_hi, "dp", axis=0, tiled=True)
    nt = (((1,), (1,)), ((), ()))
    hidden_term = (
        lax.dot_general(grad_lo, weight_lo, nt, preferred_element_type=f32)
        + lax.dot_general(grad_hi, weight_hi, nt, preferred_element_type=f32)
    ).astype(bf16)
    feats = hidden_term.shape[1] // n_vocab
    terms = hidden_term.reshape(rows, n_vocab, feats).swapaxes(0, 1)
    terms = lax.all_to_all(terms, "vocab", 0, 0, tiled=True)
    hidden_grad = jnp.sum(terms.astype(f32), axis=0).astype(bf16)
    objectives = to_all(jnp.full((8, 128), group_objective, f32), "dp").reshape(n_dp, 8, 128)
    loss_value = jnp.sum(objectives[:, 0, 0]) / (rows * n_dp)
    grad_cols = lax.all_to_all(rows_full, "dp", split_axis=1, concat_axis=0, tiled=True)
    tn = (((0,), (0,)), ((), ()))
    head_grad = jnp.concatenate(
        [
            lax.dot_general(grad_cols, all_lo, tn, preferred_element_type=f32),
            lax.dot_general(grad_cols, all_hi, tn, preferred_element_type=f32),
        ],
        axis=1,
    )
    return (hidden_grad, head_grad, loss_value)


def solution(mesh):
    return jax.shard_map(
        on_device,
        mesh=mesh,
        in_specs=(
            P("dp", "vocab"),
            P("dp", "vocab"),
            P("dp", "vocab"),
            P("dp"),
            P("dp", None),
            P("dp", None),
        ),
        out_specs=(P("dp", "vocab"), P("dp", "vocab"), P()),
        check_vma=False,
    )
```

```python
import jax
import jax.numpy as jnp
from jax import lax
from jax.experimental import pallas as pl
from jax.experimental.pallas import tpu as pltpu
from jax.sharding import PartitionSpec as P

dpo_beta = 0.1
dpo_gamma = 4.0


def pair_weights(log_ratio, segments, ordering):
    seq_count = ordering.shape[0]
    labels = lax.broadcasted_iota(jnp.int32, (1, seq_count), 1)
    seq_hot = (segments[:, None] == labels).astype(jnp.float32)
    seq_ratio = jnp.sum(seq_hot * log_ratio[:, None], axis=0)
    chosen = ordering[0::2]
    rejected = ordering[1::2]
    chosen_hot = (chosen[:, None] == labels).astype(jnp.float32)
    rejected_hot = (rejected[:, None] == labels).astype(jnp.float32)
    margin = dpo_beta * (
        jnp.sum(chosen_hot * seq_ratio[None, :], axis=1)
        - jnp.sum(rejected_hot * seq_ratio[None, :], axis=1)
    )
    strength = dpo_gamma * dpo_beta * jax.nn.sigmoid(-margin)
    coeffs = jnp.sum((rejected_hot - chosen_hot) * strength[:, None], axis=0)
    row_weight = jnp.sum(seq_hot * coeffs[None, :], axis=1)
    return (row_weight, jnp.sum(jax.nn.softplus(-margin)))


def to_all(block, axis, groups=None):
    count = lax.axis_size(axis) if groups is None else len(groups[0])
    copies = jnp.broadcast_to(block[None], (count,) + block.shape)
    return lax.all_to_all(copies, axis, 0, 0, axis_index_groups=groups, tiled=True)


def head_kernel(core_ref, objective_ref, own_ref, other_ref, grad_ref, out_ref):
    f32, bf16 = jnp.float32, jnp.bfloat16
    grad = grad_ref[...]
    own = jnp.dot(own_ref[...], grad, preferred_element_type=f32).astype(bf16)
    other = jnp.dot(other_ref[...], grad, preferred_element_type=f32).astype(bf16)
    blocks, tall, _ = out_ref.shape
    feats = own.shape[0] // blocks
    extra = tall - 2 * feats
    value = jnp.full((extra, own.shape[1]), objective_ref[0], f32)
    high = value.astype(bf16).astype(f32)
    middle = (value - high).astype(bf16).astype(f32)
    low = value - high - middle
    line = lax.broadcasted_iota(jnp.int32, value.shape, 0)
    pieces = jnp.where(line == 0, high, jnp.where(line == 1, middle, jnp.where(line == 2, low, 0.0)))
    pieces = pieces.astype(bf16)

    def store(first, second):
        for j in range(blocks):
            out_ref[j, :feats] = first[j * feats : (j + 1) * feats]
            out_ref[j, feats : 2 * feats] = second[j * feats : (j + 1) * feats]
            out_ref[j, 2 * feats :] = pieces

    @pl.when(core_ref[0] == 0)
    def _():
        store(own, other)

    @pl.when(core_ref[0] != 0)
    def _():
        store(other, own)


def head_partial(core, objective, own, other, grad, blocks, extra):
    tall, rows = own.shape
    cols = grad.shape[1]
    steps = 4
    per = blocks // steps
    feats = tall // blocks
    return pl.pallas_call(
        head_kernel,
        out_shape=jax.ShapeDtypeStruct((blocks, 2 * feats + extra, cols), jnp.bfloat16),
        grid=(steps,),
        in_specs=[
            pl.BlockSpec(memory_space=pltpu.SMEM),
            pl.BlockSpec(memory_space=pltpu.SMEM),
            pl.BlockSpec((tall // steps, rows), lambda i: (i, 0)),
            pl.BlockSpec((tall // steps, rows), lambda i: (i, 0)),
            pl.BlockSpec((rows, cols), lambda i: (0, 0)),
        ],
        out_specs=pl.BlockSpec((per, 2 * feats + extra, cols), lambda i: (i, 0, 0)),
        compiler_params=pltpu.CompilerParams(vmem_limit_bytes=32 * 1024 * 1024),
        cost_estimate=pl.CostEstimate(
            flops=4 * tall * rows * cols,
            bytes_accessed=4 * tall * rows + 2 * rows * cols + 4 * tall * cols,
            transcendentals=0,
        ),
    )(core, objective, own, other, grad)


def unpack_kernel(parts_ref, grad_ref, total_ref):
    f32 = jnp.float32
    count, _, cols = parts_ref.shape
    tall = grad_ref.shape[0]
    for j in range(count):
        grad_ref[:, j * cols : (j + 1) * cols] = parts_ref[j, :tall].astype(f32)
    lines = jnp.sum(parts_ref[:, tall:].astype(f32), axis=0)
    total_ref[0] = jnp.sum(lines[:3, :1])


def unpack(parts, tall):
    count, _, cols = parts.shape
    return pl.pallas_call(
        unpack_kernel,
        out_shape=(
            jax.ShapeDtypeStruct((tall, count * cols), jnp.float32),
            jax.ShapeDtypeStruct((1,), jnp.float32),
        ),
        out_specs=(pl.BlockSpec(memory_space=pltpu.VMEM), pl.BlockSpec(memory_space=pltpu.SMEM)),
        compiler_params=pltpu.CompilerParams(vmem_limit_bytes=16 * 1024 * 1024),
    )(parts)


def on_device(hidden, head_weight, teacher_logits, target_ids, segment_ids, pair_order):
    f32, bf16 = jnp.float32, jnp.bfloat16
    n_vocab = lax.axis_size("vocab")
    n_dp = lax.axis_size("dp")
    rows, feats = hidden.shape
    width = head_weight.shape[1]
    pairs = n_vocab // 2
    core = lax.axis_index("vocab") % 2
    same_core = [[2 * j + c for j in range(pairs)] for c in range(2)]
    swap = [(i, i ^ 1) for i in range(n_vocab)]
    weight_full = lax.all_gather(head_weight, "dp", axis=0, tiled=True)
    by_group = to_all(hidden.T, "dp").reshape(n_dp, feats, rows)
    by_pair = to_all(by_group, "vocab", same_core).reshape(pairs, n_dp, feats, rows)
    mine = lax.dynamic_index_in_dim(by_pair, lax.axis_index("dp"), 1, keepdims=False)
    theirs = lax.ppermute(mine, "vocab", swap)
    rows_t = jnp.stack(
        [jnp.where(core == 0, mine, theirs), jnp.where(core == 0, theirs, mine)], axis=1
    ).reshape(n_vocab * feats, rows)
    own_t = by_pair.swapaxes(1, 2).reshape(pairs * feats, n_dp * rows)
    other_t = lax.ppermute(own_t, "vocab", swap)
    tn = (((0,), (0,)), ((), ()))
    nt = (((1,), (1,)), ((), ()))
    student = lax.dot_general(rows_t, weight_full, tn, preferred_element_type=f32)
    teacher = teacher_logits.astype(f32)
    offset = lax.axis_index("vocab") * width
    column = lax.broadcasted_iota(jnp.int32, student.shape, 1) + offset
    is_target = column == target_ids[:, None]
    own_max = jnp.max(student, axis=1)
    own_tmax = jnp.max(teacher, axis=1)
    own_exp = jnp.exp(student - own_max[:, None])
    own_texp = jnp.exp(teacher - own_tmax[:, None])
    stats = jnp.stack(
        [
            own_max,
            own_tmax,
            jnp.sum(own_exp, axis=1),
            jnp.sum(own_texp, axis=1),
            jnp.sum(own_texp * (teacher - student), axis=1),
            jnp.sum(jnp.where(is_target, student, 0.0), axis=1),
            jnp.sum(jnp.where(is_target, teacher, 0.0), axis=1),
            jnp.zeros((rows,), f32),
        ]
    )
    every = to_all(stats, "vocab").reshape(n_vocab, 8, rows)
    max_student = jnp.max(every[:, 0], axis=0)
    max_teacher = jnp.max(every[:, 1], axis=0)
    scale_s = jnp.exp(every[:, 0] - max_student[None])
    scale_t = jnp.exp(every[:, 1] - max_teacher[None])
    sum_student = jnp.sum(every[:, 2] * scale_s, axis=0)
    sum_teacher = jnp.sum(every[:, 3] * scale_t, axis=0)
    cross = jnp.sum(every[:, 4] * scale_t, axis=0)
    target_student = jnp.sum(every[:, 5], axis=0)
    target_teacher = jnp.sum(every[:, 6], axis=0)
    lse_student = max_student + jnp.log(sum_student)
    lse_teacher = max_teacher + jnp.log(sum_teacher)
    kl_rows = cross / sum_teacher - lse_teacher + lse_student
    log_ratio = target_student - lse_student - (target_teacher - lse_teacher)
    row_weight, dpo_sum = pair_weights(log_ratio, segment_ids[0], pair_order[0])
    group_objective = jnp.sum(kl_rows) + dpo_gamma * dpo_sum
    exp_student = jnp.exp(student - max_student[:, None])
    exp_teacher = jnp.exp(teacher - max_teacher[:, None])
    prob_student = exp_student / sum_student[:, None]
    prob_teacher = exp_teacher / sum_teacher[:, None]
    logit_grad = (
        prob_student
        - prob_teacher
        + row_weight[:, None] * (is_target.astype(f32) - prob_student)
    ).astype(bf16)
    chunk = width // n_dp
    chunks = logit_grad.reshape(rows, n_dp, chunk).swapaxes(0, 1)
    chunks = lax.all_to_all(chunks, "dp", 0, 0, tiled=True)
    hidden_term = lax.dot_general(logit_grad, weight_full, nt, preferred_element_type=f32)
    terms = hidden_term.astype(bf16).reshape(rows, n_vocab, feats).swapaxes(0, 1)
    chunks, terms = lax.optimization_barrier((chunks, terms))
    partial = head_partial(
        core.astype(jnp.int32).reshape(1),
        group_objective.reshape(1),
        own_t,
        other_t,
        chunks.reshape(n_dp * rows, chunk),
        pairs,
        16,
    )
    terms = lax.all_to_all(terms, "vocab", 0, 0, tiled=True)
    hidden_grad = jnp.sum(terms.astype(f32), axis=0).astype(bf16)
    partial, hidden_grad = lax.optimization_barrier((partial, hidden_grad))
    parts = lax.all_to_all(partial, "dp", 0, 0, tiled=True)
    head_grad, total = unpack(parts, 2 * feats)
    loss_value = total[0] / (rows * n_dp)
    return (hidden_grad, head_grad, loss_value)


def solution(mesh):
    return jax.shard_map(
        on_device,
        mesh=mesh,
        in_specs=(
            P("dp", "vocab"),
            P("dp", "vocab"),
            P("dp", "vocab"),
            P("dp"),
            P("dp", None),
            P("dp", None),
        ),
        out_specs=(P("dp", "vocab"), P("dp", "vocab"), P()),
        check_vma=False,
    )
```

```python
import jax
import jax.numpy as jnp
from jax import lax
from jax.experimental import pallas as pl
from jax.experimental.pallas import tpu as pltpu
from jax.sharding import PartitionSpec as P

dpo_beta = 0.1
dpo_gamma = 4.0


def pair_signs(segments, ordering):
    count = ordering.shape[0]
    labels = lax.broadcasted_iota(jnp.int32, (count, 1), 0)
    seq_hot = (segments[None, :] == labels).astype(jnp.float32)
    chosen = (labels == ordering[None, 0::2]).astype(jnp.float32)
    rejected = (labels == ordering[None, 1::2]).astype(jnp.float32)
    side = chosen - rejected
    pair = chosen + rejected
    margin_sign = jnp.sum(pair[:, None, :] * side[None, :, :], axis=2)
    into_margin = jnp.sum(margin_sign[:, :, None] * seq_hot[None, :, :], axis=1)
    into_weight = jnp.sum(side, axis=1)[:, None] * seq_hot
    return into_margin, into_weight


def to_all(block, axis, groups=None):
    count = lax.axis_size(axis) if groups is None else len(groups[0])
    copies = jnp.broadcast_to(block[None], (count,) + block.shape)
    return lax.all_to_all(copies, axis, 0, 0, axis_index_groups=groups, tiled=True)


def relayout_kernel(in_ref, out_ref):
    groups, _, rows = in_ref.shape[1:]
    for j in range(groups):
        out_ref[:, j * rows : (j + 1) * rows] = in_ref[0, j]


def relayout(by_pair):
    pairs, groups, feats, rows = by_pair.shape
    return pl.pallas_call(
        relayout_kernel,
        out_shape=jax.ShapeDtypeStruct((pairs * feats, groups * rows), by_pair.dtype),
        grid=(pairs,),
        in_specs=[pl.BlockSpec((1, groups, feats, rows), lambda i: (i, 0, 0, 0))],
        out_specs=pl.BlockSpec((feats, groups * rows), lambda i: (i, 0)),
        compiler_params=pltpu.CompilerParams(vmem_limit_bytes=16 * 1024 * 1024),
        cost_estimate=pl.CostEstimate(flops=0, bytes_accessed=4 * by_pair.size, transcendentals=0),
    )(by_pair)


def grad_kernel(
    every_ref, student_ref, teacher_ref, target_ref, margin_ref, weight_ref,
    grad_ref, gathered_ref, chunks_ref, objective_ref,
):
    f32, bf16 = jnp.float32, jnp.bfloat16
    maxes_s, maxes_t = every_ref[:, 0, :], every_ref[:, 1, :]
    max_s = jnp.max(maxes_s, axis=0, keepdims=True)
    max_t = jnp.max(maxes_t, axis=0, keepdims=True)
    scale_s = jnp.exp(maxes_s - max_s)
    scale_t = jnp.exp(maxes_t - max_t)
    sum_s = jnp.sum(every_ref[:, 2, :] * scale_s, axis=0, keepdims=True)
    sum_t = jnp.sum(every_ref[:, 3, :] * scale_t, axis=0, keepdims=True)
    cross = jnp.sum(every_ref[:, 4, :] * scale_t, axis=0, keepdims=True)
    target_s = jnp.sum(every_ref[:, 5, :], axis=0, keepdims=True)
    target_t = jnp.sum(every_ref[:, 6, :], axis=0, keepdims=True)
    lse_s = max_s + jnp.log(sum_s)
    lse_t = max_t + jnp.log(sum_t)
    kl = cross / sum_t - lse_t + lse_s
    log_ratio = target_s - lse_s - (target_t - lse_t)
    margin = dpo_beta * jnp.sum(margin_ref[...] * log_ratio, axis=1, keepdims=True)
    strength = dpo_gamma * dpo_beta / (1.0 + jnp.exp(margin))
    weight = -jnp.sum(weight_ref[...] * strength, axis=0, keepdims=True)
    dpo = jnp.maximum(-margin, 0.0) + jnp.log(1.0 + jnp.exp(-jnp.abs(margin)))
    objective_ref[0] = jnp.sum(kl) + 0.5 * dpo_gamma * jnp.sum(dpo)
    lines = jnp.concatenate(
        [max_s, 1.0 / sum_s, max_t, 1.0 / sum_t, weight, weight, weight, weight], axis=0
    )
    columns = jnp.transpose(lines)
    max_s, inv_s = columns[:, 0:1], columns[:, 1:2]
    max_t, inv_t, weight = columns[:, 2:3], columns[:, 3:4], columns[:, 4:5]
    target = target_ref[...]
    rows, width = student_ref.shape
    split = gathered_ref.shape[1]
    step = 256
    for low in range(0, width, step):
        prob_s = jnp.exp(student_ref[:, low : low + step] - max_s) * inv_s
        prob_t = jnp.exp(teacher_ref[:, low : low + step].astype(f32) - max_t) * inv_t
        column = lax.broadcasted_iota(jnp.int32, (rows, step), 1) + low
        hot = jnp.where(column == target, 1.0, 0.0)
        grad = prob_s - prob_t + weight * (hot - prob_s)
        rounded = grad.astype(bf16)
        grad_ref[:, low : low + step] = rounded
        if low < split:
            gathered_ref[:, low : low + step] = rounded
        else:
            chunks_ref[low - split : low - split + step, :] = jnp.transpose(grad).astype(bf16)


def make_grad(every, student, teacher, target, into_margin, into_weight, split):
    rows, width = student.shape
    f32, bf16 = jnp.float32, jnp.bfloat16
    vmem = pl.BlockSpec(memory_space=pltpu.VMEM)
    return pl.pallas_call(
        grad_kernel,
        out_shape=(
            jax.ShapeDtypeStruct((rows, width), bf16),
            jax.ShapeDtypeStruct((rows, split), bf16),
            jax.ShapeDtypeStruct((width - split, rows), bf16),
            jax.ShapeDtypeStruct((1,), f32),
        ),
        out_specs=(vmem, vmem, vmem, pl.BlockSpec(memory_space=pltpu.SMEM)),
        compiler_params=pltpu.CompilerParams(vmem_limit_bytes=32 * 1024 * 1024),
    )(every, student, teacher, target, into_margin, into_weight)


def head_kernel(core_ref, objective_ref, own_ref, other_ref, grad_ref, out_ref, wide_ref):
    f32, bf16 = jnp.float32, jnp.bfloat16
    groups, chunk, rows = grad_ref.shape

    @pl.when(pl.program_id(0) == 0)
    def _():
        for z in range(groups):
            wide_ref[:, z * rows : (z + 1) * rows] = grad_ref[z]

    nt = (((1,), (1,)), ((), ()))
    wide = wide_ref[...]
    own = lax.dot_general(wide, own_ref[...], nt, preferred_element_type=f32)
    other = lax.dot_general(wide, other_ref[...], nt, preferred_element_type=f32)
    is_first = core_ref[0] == 0
    first = jnp.where(is_first, own, other)
    second = jnp.where(is_first, other, own)
    blocks, tall, lanes = out_ref.shape
    half = lanes // 2
    value = jnp.full((tall - chunk, lanes), objective_ref[0], f32)
    high = value.astype(bf16).astype(f32)
    middle = (value - high).astype(bf16).astype(f32)
    low = value - high - middle
    line = lax.broadcasted_iota(jnp.int32, value.shape, 0)
    pieces = jnp.where(line == 0, high, jnp.where(line == 1, middle, jnp.where(line == 2, low, 0.0)))
    pieces = pieces.astype(bf16)
    left = lax.broadcasted_iota(jnp.int32, (chunk, lanes), 1) < half
    for j in range(0, blocks, 2):
        front = first[:, j * half : j * half + lanes]
        back = second[:, j * half : j * half + lanes]
        out_ref[j, :chunk] = jnp.where(left, front, pltpu.roll(back, half, 1)).astype(bf16)
        out_ref[j + 1, :chunk] = jnp.where(left, pltpu.roll(front, half, 1), back).astype(bf16)
        out_ref[j, chunk:] = pieces
        out_ref[j + 1, chunk:] = pieces


def head_partial(core, objective, own, other, grad, blocks, extra):
    tall, all_rows = own.shape
    groups, chunk, rows = grad.shape
    steps = 4
    per = blocks // steps
    lanes = 2 * tall // blocks
    return pl.pallas_call(
        head_kernel,
        out_shape=jax.ShapeDtypeStruct((blocks, chunk + extra, lanes), jnp.bfloat16),
        grid=(steps,),
        in_specs=[
            pl.BlockSpec(memory_space=pltpu.SMEM),
            pl.BlockSpec(memory_space=pltpu.SMEM),
            pl.BlockSpec((tall // steps, all_rows), lambda i: (i, 0)),
            pl.BlockSpec((tall // steps, all_rows), lambda i: (i, 0)),
            pl.BlockSpec((groups, chunk, rows), lambda i: (0, 0, 0)),
        ],
        out_specs=pl.BlockSpec((per, chunk + extra, lanes), lambda i: (i, 0, 0)),
        scratch_shapes=[pltpu.VMEM((chunk, all_rows), jnp.bfloat16)],
        compiler_params=pltpu.CompilerParams(vmem_limit_bytes=32 * 1024 * 1024),
        cost_estimate=pl.CostEstimate(
            flops=4 * tall * all_rows * chunk,
            bytes_accessed=4 * tall * all_rows + 2 * all_rows * chunk + 4 * tall * chunk,
            transcendentals=0,
        ),
    )(core, objective, own, other, grad)


def finish_kernel(hidden_ref, gathered_ref, parts_ref, grad_ref, total_ref, stack_ref):
    f32 = jnp.float32
    count, tall, feats = parts_ref.shape
    step = gathered_ref.shape[1]
    i = pl.program_id(0)
    low = pl.multiple_of(i * step, step)
    grad_ref[:, pl.ds(low, step)] = jnp.dot(
        hidden_ref[...], gathered_ref[...], preferred_element_type=f32
    )

    @pl.when(i == 0)
    def _():
        chunk = stack_ref.shape[0] // count
        split = grad_ref.shape[1] - stack_ref.shape[0]
        for j in range(count):
            stack_ref[j * chunk : (j + 1) * chunk] = parts_ref[j, :chunk].astype(f32)
        for j in range(0, count * chunk, feats):
            grad_ref[:, split + j : split + j + feats] = jnp.transpose(stack_ref[j : j + feats])
        lines = jnp.sum(parts_ref[:, chunk:].astype(f32), axis=0)
        total_ref[0] = jnp.sum(lines[:3, :1])


def finish(hidden_slab, gathered, parts, extra):
    feats, all_rows = hidden_slab.shape
    split = gathered.shape[1]
    count, tall, _ = parts.shape
    chunk = tall - extra
    step = 256
    width = split + count * chunk
    return pl.pallas_call(
        finish_kernel,
        out_shape=(
            jax.ShapeDtypeStruct((feats, width), jnp.float32),
            jax.ShapeDtypeStruct((1,), jnp.float32),
        ),
        grid=(split // step,),
        in_specs=[
            pl.BlockSpec((feats, all_rows), lambda i: (0, 0)),
            pl.BlockSpec((all_rows, step), lambda i: (0, i)),
            pl.BlockSpec((count, tall, feats), lambda i: (0, 0, 0)),
        ],
        out_specs=(
            pl.BlockSpec((feats, width), lambda i: (0, 0)),
            pl.BlockSpec(memory_space=pltpu.SMEM),
        ),
        scratch_shapes=[pltpu.VMEM((count * chunk, feats), jnp.float32)],
        compiler_params=pltpu.CompilerParams(vmem_limit_bytes=32 * 1024 * 1024),
    )(hidden_slab, gathered, parts)


def on_device(hidden, head_weight, teacher_logits, target_ids, segment_ids, pair_order):
    f32, bf16 = jnp.float32, jnp.bfloat16
    n_vocab = lax.axis_size("vocab")
    n_dp = lax.axis_size("dp")
    rows, feats = hidden.shape
    width = head_weight.shape[1]
    pairs = n_vocab // 2
    core = lax.axis_index("vocab") % 2
    same_core = [[2 * j + c for j in range(pairs)] for c in range(2)]
    swap = [(i, i ^ 1) for i in range(n_vocab)]
    weight_full = lax.all_gather(head_weight, "dp", axis=0, tiled=True)
    by_group = to_all(hidden.T, "dp").reshape(n_dp, feats, rows)
    by_pair = to_all(by_group, "vocab", same_core).reshape(pairs, n_dp, feats, rows)
    own_t = relayout(by_pair)
    other_t = lax.ppermute(own_t, "vocab", swap)
    place = lax.axis_index("dp")

    def by_core(own, other, axis):
        return jnp.stack([jnp.where(core == 0, own, other), jnp.where(core == 0, other, own)], axis=axis)

    mine = lax.dynamic_slice_in_dim(own_t, place * rows, rows, 1).reshape(pairs, feats, rows)
    theirs = lax.dynamic_slice_in_dim(other_t, place * rows, rows, 1).reshape(pairs, feats, rows)
    rows_t = by_core(mine, theirs, 1).reshape(n_vocab * feats, rows)
    slab = by_core(
        lax.dynamic_slice_in_dim(own_t, place * feats, feats, 0),
        lax.dynamic_slice_in_dim(other_t, place * feats, feats, 0),
        0,
    ).reshape(2 * feats, n_dp * rows)
    into_margin, into_weight = pair_signs(segment_ids[0], pair_order[0])
    tn = (((0,), (0,)), ((), ()))
    nt = (((1,), (1,)), ((), ()))
    student = lax.dot_general(rows_t, weight_full, tn, preferred_element_type=f32)
    teacher = teacher_logits.astype(f32)
    offset = lax.axis_index("vocab") * width
    column = lax.broadcasted_iota(jnp.int32, student.shape, 1) + offset
    is_target = column == target_ids[:, None]
    own_max = jnp.max(student, axis=1)
    own_tmax = jnp.max(teacher, axis=1)
    own_exp = jnp.exp(student - own_max[:, None])
    own_texp = jnp.exp(teacher - own_tmax[:, None])
    stats = jnp.stack(
        [
            own_max,
            own_tmax,
            jnp.sum(own_exp, axis=1),
            jnp.sum(own_texp, axis=1),
            jnp.sum(own_texp * (teacher - student), axis=1),
            jnp.sum(jnp.where(is_target, student, 0.0), axis=1),
            jnp.sum(jnp.where(is_target, teacher, 0.0), axis=1),
            jnp.zeros((rows,), f32),
        ]
    )
    every = to_all(stats, "vocab").reshape(n_vocab, 8, rows)
    split = 3 * width // 8
    extra = 16
    logit_grad, gathered, chunks, objective = make_grad(
        every, student, teacher_logits, (target_ids - offset)[:, None], into_margin, into_weight, split
    )
    gathered = lax.all_gather(gathered, "dp", axis=0, tiled=True)
    chunks = chunks.reshape(n_dp, (width - split) // n_dp, rows)
    chunks = lax.all_to_all(chunks, "dp", 0, 0, tiled=True)
    hidden_term = lax.dot_general(logit_grad, weight_full, nt, preferred_element_type=f32)
    terms = hidden_term.astype(bf16).reshape(rows, n_vocab, feats).swapaxes(0, 1)
    chunks, terms = lax.optimization_barrier((chunks, terms))
    partial = head_partial(
        core.astype(jnp.int32).reshape(1), objective, own_t, other_t, chunks, pairs, extra
    )
    terms = lax.all_to_all(terms, "vocab", 0, 0, tiled=True)
    hidden_grad = jnp.sum(terms.astype(f32), axis=0).astype(bf16)
    partial, hidden_grad = lax.optimization_barrier((partial, hidden_grad))
    parts = lax.all_to_all(partial, "dp", 0, 0, tiled=True)
    head_grad, total = finish(slab, gathered, parts, extra)
    loss_value = total[0] / (rows * n_dp)
    return (hidden_grad, head_grad, loss_value)


def solution(mesh):
    return jax.shard_map(
        on_device,
        mesh=mesh,
        in_specs=(
            P("dp", "vocab"),
            P("dp", "vocab"),
            P("dp", "vocab"),
            P("dp"),
            P("dp", None),
            P("dp", None),
        ),
        out_specs=(P("dp", "vocab"), P("dp", "vocab"), P()),
        check_vma=False,
    )
```

```python
import jax
import jax.numpy as jnp
from jax import lax
from jax.experimental import pallas as pl
from jax.experimental.pallas import tpu as pltpu
from jax.sharding import PartitionSpec as P

dpo_beta = 0.1
dpo_gamma = 4.0


def pair_signs(segments, ordering):
    count = ordering.shape[0]
    labels = lax.broadcasted_iota(jnp.int32, (count, 1), 0)
    seq_hot = (segments[None, :] == labels).astype(jnp.float32)
    chosen = (labels == ordering[None, 0::2]).astype(jnp.float32)
    rejected = (labels == ordering[None, 1::2]).astype(jnp.float32)
    side = chosen - rejected
    pair = chosen + rejected
    margin_sign = jnp.sum(pair[:, None, :] * side[None, :, :], axis=2)
    into_margin = jnp.sum(margin_sign[:, :, None] * seq_hot[None, :, :], axis=1)
    into_weight = jnp.sum(side, axis=1)[:, None] * seq_hot
    return into_margin, into_weight


def to_all(block, axis, groups=None):
    count = lax.axis_size(axis) if groups is None else len(groups[0])
    copies = jnp.broadcast_to(block[None], (count,) + block.shape)
    return lax.all_to_all(copies, axis, 0, 0, axis_index_groups=groups, tiled=True)


def relayout_kernel(in_ref, out_ref):
    groups, _, rows = in_ref.shape[1:]
    for j in range(groups):
        out_ref[:, j * rows : (j + 1) * rows] = in_ref[0, j]


def relayout(by_pair):
    pairs, groups, feats, rows = by_pair.shape
    return pl.pallas_call(
        relayout_kernel,
        out_shape=jax.ShapeDtypeStruct((pairs * feats, groups * rows), by_pair.dtype),
        grid=(pairs,),
        in_specs=[pl.BlockSpec((1, groups, feats, rows), lambda i: (i, 0, 0, 0))],
        out_specs=pl.BlockSpec((feats, groups * rows), lambda i: (i, 0)),
        compiler_params=pltpu.CompilerParams(vmem_limit_bytes=16 * 1024 * 1024),
        cost_estimate=pl.CostEstimate(flops=0, bytes_accessed=4 * by_pair.size, transcendentals=0),
    )(by_pair)


def grad_kernel(
    every_ref, student_ref, teacher_ref, target_ref, margin_ref, weight_ref,
    grad_ref, gathered_ref, chunks_ref, objective_ref,
):
    f32, bf16 = jnp.float32, jnp.bfloat16
    maxes_s, maxes_t = every_ref[:, 0, :], every_ref[:, 1, :]
    max_s = jnp.max(maxes_s, axis=0, keepdims=True)
    max_t = jnp.max(maxes_t, axis=0, keepdims=True)
    scale_s = jnp.exp(maxes_s - max_s)
    scale_t = jnp.exp(maxes_t - max_t)
    sum_s = jnp.sum(every_ref[:, 2, :] * scale_s, axis=0, keepdims=True)
    sum_t = jnp.sum(every_ref[:, 3, :] * scale_t, axis=0, keepdims=True)
    cross = jnp.sum(every_ref[:, 4, :] * scale_t, axis=0, keepdims=True)
    target_s = jnp.sum(every_ref[:, 5, :], axis=0, keepdims=True)
    target_t = jnp.sum(every_ref[:, 6, :], axis=0, keepdims=True)
    lse_s = max_s + jnp.log(sum_s)
    lse_t = max_t + jnp.log(sum_t)
    kl = cross / sum_t - lse_t + lse_s
    log_ratio = target_s - lse_s - (target_t - lse_t)
    margin = dpo_beta * jnp.sum(margin_ref[...] * log_ratio, axis=1, keepdims=True)
    strength = dpo_gamma * dpo_beta / (1.0 + jnp.exp(margin))
    weight = -jnp.sum(weight_ref[...] * strength, axis=0, keepdims=True)
    dpo = jnp.maximum(-margin, 0.0) + jnp.log(1.0 + jnp.exp(-jnp.abs(margin)))
    objective_ref[0] = jnp.sum(kl) + 0.5 * dpo_gamma * jnp.sum(dpo)
    lines = jnp.concatenate(
        [max_s, 1.0 / sum_s, max_t, 1.0 / sum_t, weight, weight, weight, weight], axis=0
    )
    columns = jnp.transpose(lines)
    max_s, inv_s = columns[:, 0:1], columns[:, 1:2]
    max_t, inv_t, weight = columns[:, 2:3], columns[:, 3:4], columns[:, 4:5]
    target = target_ref[...]
    rows, width = student_ref.shape
    split = gathered_ref.shape[1]
    step = 256
    for low in range(0, width, step):
        prob_s = jnp.exp(student_ref[:, low : low + step] - max_s) * inv_s
        prob_t = jnp.exp(teacher_ref[:, low : low + step].astype(f32) - max_t) * inv_t
        column = lax.broadcasted_iota(jnp.int32, (rows, step), 1) + low
        hot = jnp.where(column == target, 1.0, 0.0)
        grad = prob_s - prob_t + weight * (hot - prob_s)
        rounded = grad.astype(bf16)
        grad_ref[:, low : low + step] = rounded
        if low < split:
            gathered_ref[:, low : low + step] = rounded
        else:
            chunks_ref[low - split : low - split + step, :] = jnp.transpose(grad).astype(bf16)


def make_grad(every, student, teacher, target, into_margin, into_weight, split):
    rows, width = student.shape
    f32, bf16 = jnp.float32, jnp.bfloat16
    vmem = pl.BlockSpec(memory_space=pltpu.VMEM)
    return pl.pallas_call(
        grad_kernel,
        out_shape=(
            jax.ShapeDtypeStruct((rows, width), bf16),
            jax.ShapeDtypeStruct((rows, split), bf16),
            jax.ShapeDtypeStruct((width - split, rows), bf16),
            jax.ShapeDtypeStruct((1,), f32),
        ),
        out_specs=(vmem, vmem, vmem, pl.BlockSpec(memory_space=pltpu.SMEM)),
        compiler_params=pltpu.CompilerParams(vmem_limit_bytes=32 * 1024 * 1024),
    )(every, student, teacher, target, into_margin, into_weight)


def head_kernel(core_ref, objective_ref, own_ref, other_ref, grad_ref, out_ref, tall_ref):
    f32, bf16 = jnp.float32, jnp.bfloat16
    groups, chunk, rows = grad_ref.shape

    @pl.when(pl.program_id(0) == 0)
    def _():
        for z in range(groups):
            tall_ref[z * rows : (z + 1) * rows] = jnp.transpose(grad_ref[z].astype(f32)).astype(bf16)

    grad = tall_ref[...]
    own = jnp.transpose(jnp.dot(own_ref[...], grad, preferred_element_type=f32))
    other = jnp.transpose(jnp.dot(other_ref[...], grad, preferred_element_type=f32))
    is_first = core_ref[0] == 0
    first = jnp.where(is_first, own, other)
    second = jnp.where(is_first, other, own)
    blocks, tall, lanes = out_ref.shape
    half = lanes // 2
    value = jnp.full((tall - chunk, lanes), objective_ref[0], f32)
    high = value.astype(bf16).astype(f32)
    middle = (value - high).astype(bf16).astype(f32)
    low = value - high - middle
    line = lax.broadcasted_iota(jnp.int32, value.shape, 0)
    pieces = jnp.where(line == 0, high, jnp.where(line == 1, middle, jnp.where(line == 2, low, 0.0)))
    pieces = pieces.astype(bf16)
    left = lax.broadcasted_iota(jnp.int32, (chunk, lanes), 1) < half
    for j in range(0, blocks, 2):
        front = first[:, j * half : j * half + lanes]
        back = second[:, j * half : j * half + lanes]
        out_ref[j, :chunk] = jnp.where(left, front, pltpu.roll(back, half, 1)).astype(bf16)
        out_ref[j + 1, :chunk] = jnp.where(left, pltpu.roll(front, half, 1), back).astype(bf16)
        out_ref[j, chunk:] = pieces
        out_ref[j + 1, chunk:] = pieces


def head_partial(core, objective, own, other, grad, blocks, extra):
    tall, all_rows = own.shape
    groups, chunk, rows = grad.shape
    steps = 4
    per = blocks // steps
    lanes = 2 * tall // blocks
    return pl.pallas_call(
        head_kernel,
        out_shape=jax.ShapeDtypeStruct((blocks, chunk + extra, lanes), jnp.bfloat16),
        grid=(steps,),
        in_specs=[
            pl.BlockSpec(memory_space=pltpu.SMEM),
            pl.BlockSpec(memory_space=pltpu.SMEM),
            pl.BlockSpec((tall // steps, all_rows), lambda i: (i, 0)),
            pl.BlockSpec((tall // steps, all_rows), lambda i: (i, 0)),
            pl.BlockSpec((groups, chunk, rows), lambda i: (0, 0, 0)),
        ],
        out_specs=pl.BlockSpec((per, chunk + extra, lanes), lambda i: (i, 0, 0)),
        scratch_shapes=[pltpu.VMEM((all_rows, chunk), jnp.bfloat16)],
        compiler_params=pltpu.CompilerParams(vmem_limit_bytes=32 * 1024 * 1024),
        cost_estimate=pl.CostEstimate(
            flops=4 * tall * all_rows * chunk,
            bytes_accessed=4 * tall * all_rows + 2 * all_rows * chunk + 4 * tall * chunk,
            transcendentals=0,
        ),
    )(core, objective, own, other, grad)


def finish_kernel(hidden_ref, gathered_ref, parts_ref, grad_ref, total_ref, stack_ref):
    f32 = jnp.float32
    count, tall, feats = parts_ref.shape
    step = gathered_ref.shape[1]
    i = pl.program_id(0)
    low = pl.multiple_of(i * step, step)
    grad_ref[:, pl.ds(low, step)] = jnp.dot(
        hidden_ref[...], gathered_ref[...], preferred_element_type=f32
    )

    @pl.when(i == 0)
    def _():
        chunk = stack_ref.shape[0] // count
        split = grad_ref.shape[1] - stack_ref.shape[0]
        for j in range(count):
            stack_ref[j * chunk : (j + 1) * chunk] = parts_ref[j, :chunk].astype(f32)
        for j in range(0, count * chunk, feats):
            grad_ref[:, split + j : split + j + feats] = jnp.transpose(stack_ref[j : j + feats])
        lines = jnp.sum(parts_ref[:, chunk:].astype(f32), axis=0)
        total_ref[0] = jnp.sum(lines[:3, :1])


def finish(hidden_slab, gathered, parts, extra):
    feats, all_rows = hidden_slab.shape
    split = gathered.shape[1]
    count, tall, _ = parts.shape
    chunk = tall - extra
    step = 256
    width = split + count * chunk
    return pl.pallas_call(
        finish_kernel,
        out_shape=(
            jax.ShapeDtypeStruct((feats, width), jnp.float32),
            jax.ShapeDtypeStruct((1,), jnp.float32),
        ),
        grid=(split // step,),
        in_specs=[
            pl.BlockSpec((feats, all_rows), lambda i: (0, 0)),
            pl.BlockSpec((all_rows, step), lambda i: (0, i)),
            pl.BlockSpec((count, tall, feats), lambda i: (0, 0, 0)),
        ],
        out_specs=(
            pl.BlockSpec((feats, width), lambda i: (0, 0)),
            pl.BlockSpec(memory_space=pltpu.SMEM),
        ),
        scratch_shapes=[pltpu.VMEM((count * chunk, feats), jnp.float32)],
        compiler_params=pltpu.CompilerParams(vmem_limit_bytes=56 * 1024 * 1024),
    )(hidden_slab, gathered, parts)


def on_device(hidden, head_weight, teacher_logits, target_ids, segment_ids, pair_order):
    f32, bf16 = jnp.float32, jnp.bfloat16
    n_vocab = lax.axis_size("vocab")
    n_dp = lax.axis_size("dp")
    rows, feats = hidden.shape
    width = head_weight.shape[1]
    pairs = n_vocab // 2
    core = lax.axis_index("vocab") % 2
    same_core = [[2 * j + c for j in range(pairs)] for c in range(2)]
    swap = [(i, i ^ 1) for i in range(n_vocab)]
    weight_full = lax.all_gather(head_weight, "dp", axis=0, tiled=True)
    by_group = to_all(hidden.T, "dp").reshape(n_dp, feats, rows)
    by_pair = to_all(by_group, "vocab", same_core).reshape(pairs, n_dp, feats, rows)
    own_t = relayout(by_pair)
    other_t = lax.ppermute(own_t, "vocab", swap)
    place = lax.axis_index("dp")

    def by_core(own, other, axis):
        return jnp.stack([jnp.where(core == 0, own, other), jnp.where(core == 0, other, own)], axis=axis)

    mine = lax.dynamic_slice_in_dim(own_t, place * rows, rows, 1).reshape(pairs, feats, rows)
    theirs = lax.dynamic_slice_in_dim(other_t, place * rows, rows, 1).reshape(pairs, feats, rows)
    rows_t = by_core(mine, theirs, 1).reshape(n_vocab * feats, rows)
    slab = by_core(
        lax.dynamic_slice_in_dim(own_t, place * feats, feats, 0),
        lax.dynamic_slice_in_dim(other_t, place * feats, feats, 0),
        0,
    ).reshape(2 * feats, n_dp * rows)
    into_margin, into_weight = pair_signs(segment_ids[0], pair_order[0])
    tn = (((0,), (0,)), ((), ()))
    nt = (((1,), (1,)), ((), ()))
    student = lax.dot_general(rows_t, weight_full, tn, preferred_element_type=f32)
    teacher = teacher_logits.astype(f32)
    offset = lax.axis_index("vocab") * width
    column = lax.broadcasted_iota(jnp.int32, student.shape, 1) + offset
    is_target = column == target_ids[:, None]
    own_max = jnp.max(student, axis=1)
    own_tmax = jnp.max(teacher, axis=1)
    own_exp = jnp.exp(student - own_max[:, None])
    own_texp = jnp.exp(teacher - own_tmax[:, None])
    stats = jnp.stack(
        [
            own_max,
            own_tmax,
            jnp.sum(own_exp, axis=1),
            jnp.sum(own_texp, axis=1),
            jnp.sum(own_texp * (teacher - student), axis=1),
            jnp.sum(jnp.where(is_target, student, 0.0), axis=1),
            jnp.sum(jnp.where(is_target, teacher, 0.0), axis=1),
            jnp.zeros((rows,), f32),
        ]
    )
    every = to_all(stats, "vocab").reshape(n_vocab, 8, rows)
    split = width // 4
    extra = 16
    logit_grad, gathered, chunks, objective = make_grad(
        every, student, teacher_logits, (target_ids - offset)[:, None], into_margin, into_weight, split
    )
    gathered = lax.all_gather(gathered, "dp", axis=0, tiled=True)
    chunks = chunks.reshape(n_dp, (width - split) // n_dp, rows)
    chunks = lax.all_to_all(chunks, "dp", 0, 0, tiled=True)
    hidden_term = lax.dot_general(logit_grad, weight_full, nt, preferred_element_type=f32)
    terms = hidden_term.astype(bf16).reshape(rows, n_vocab, feats).swapaxes(0, 1)
    chunks, terms = lax.optimization_barrier((chunks, terms))
    partial = head_partial(
        core.astype(jnp.int32).reshape(1), objective, own_t, other_t, chunks, pairs, extra
    )
    terms = lax.all_to_all(terms, "vocab", 0, 0, tiled=True)
    hidden_grad = jnp.sum(terms.astype(f32), axis=0).astype(bf16)
    partial, hidden_grad = lax.optimization_barrier((partial, hidden_grad))
    parts = lax.all_to_all(partial, "dp", 0, 0, tiled=True)
    head_grad, total = finish(slab, gathered, parts, extra)
    loss_value = total[0] / (rows * n_dp)
    return (hidden_grad, head_grad, loss_value)


def solution(mesh):
    return jax.shard_map(
        on_device,
        mesh=mesh,
        in_specs=(
            P("dp", "vocab"),
            P("dp", "vocab"),
            P("dp", "vocab"),
            P("dp"),
            P("dp", None),
            P("dp", None),
        ),
        out_specs=(P("dp", "vocab"), P("dp", "vocab"), P()),
        check_vma=False,
    )
```

```python
import math

import jax
import jax.numpy as jnp
from jax import lax
from jax.experimental import pallas as pl
from jax.experimental.pallas import tpu as pltpu
from jax.sharding import PartitionSpec as P

dpo_beta = 0.1
dpo_gamma = 4.0


def pair_signs(segments, ordering):
    count = ordering.shape[0]
    labels = lax.broadcasted_iota(jnp.int32, (count, 1), 0)
    seq_hot = (segments[None, :] == labels).astype(jnp.float32)
    chosen = (labels == ordering[None, 0::2]).astype(jnp.float32)
    rejected = (labels == ordering[None, 1::2]).astype(jnp.float32)
    side = chosen - rejected
    pair = chosen + rejected
    margin_sign = jnp.sum(pair[:, None, :] * side[None, :, :], axis=2)
    into_margin = jnp.sum(margin_sign[:, :, None] * seq_hot[None, :, :], axis=1)
    into_weight = jnp.sum(side, axis=1)[:, None] * seq_hot
    return into_margin, into_weight


def to_all(block, axis, groups=None):
    count = lax.axis_size(axis) if groups is None else len(groups[0])
    copies = jnp.broadcast_to(block[None], (count,) + block.shape)
    return lax.all_to_all(copies, axis, 0, 0, axis_index_groups=groups, tiled=True)


def ring_sum(terms, place, around):
    count = terms.shape[0]
    turned = lax.dynamic_slice_in_dim(jnp.concatenate([terms, terms]), place, count, 0)
    rounded = turned.astype(jnp.bfloat16)
    arrived = [lax.ppermute(rounded[d], "vocab", around[d]) for d in range(1, count)]
    return turned[0] + sum(term.astype(jnp.float32) for term in arrived)


def relayout_kernel(in_ref, out_ref):
    groups, _, rows = in_ref.shape[1:]
    for j in range(groups):
        out_ref[:, j * rows : (j + 1) * rows] = in_ref[0, j]


def relayout(by_pair):
    pairs, groups, feats, rows = by_pair.shape
    return pl.pallas_call(
        relayout_kernel,
        out_shape=jax.ShapeDtypeStruct((pairs * feats, groups * rows), by_pair.dtype),
        grid=(pairs,),
        in_specs=[pl.BlockSpec((1, groups, feats, rows), lambda i: (i, 0, 0, 0))],
        out_specs=pl.BlockSpec((feats, groups * rows), lambda i: (i, 0)),
        compiler_params=pltpu.CompilerParams(vmem_limit_bytes=16 * 1024 * 1024),
        cost_estimate=pl.CostEstimate(flops=0, bytes_accessed=4 * by_pair.size, transcendentals=0),
    )(by_pair)


def grad_kernel(
    every_ref, student_ref, teacher_ref, target_ref, margin_ref, weight_ref,
    grad_ref, chunks_ref, objective_ref,
):
    f32, bf16 = jnp.float32, jnp.bfloat16
    maxes_s, maxes_t = every_ref[:, 0, :], every_ref[:, 1, :]
    max_s = jnp.max(maxes_s, axis=0, keepdims=True)
    max_t = jnp.max(maxes_t, axis=0, keepdims=True)
    scale_s = jnp.exp(maxes_s - max_s)
    scale_t = jnp.exp(maxes_t - max_t)
    sum_s = jnp.sum(every_ref[:, 2, :] * scale_s, axis=0, keepdims=True)
    sum_t = jnp.sum(every_ref[:, 3, :] * scale_t, axis=0, keepdims=True)
    cross = jnp.sum(every_ref[:, 4, :] * scale_t, axis=0, keepdims=True)
    target_s = jnp.sum(every_ref[:, 5, :], axis=0, keepdims=True)
    target_t = jnp.sum(every_ref[:, 6, :], axis=0, keepdims=True)
    lse_s = max_s + jnp.log(sum_s)
    lse_t = max_t + jnp.log(sum_t)
    kl = cross / sum_t - lse_t + lse_s
    log_ratio = target_s - lse_s - (target_t - lse_t)
    margin = dpo_beta * jnp.sum(margin_ref[...] * log_ratio, axis=1, keepdims=True)
    strength = dpo_gamma * dpo_beta / (1.0 + jnp.exp(margin))
    weight = -jnp.sum(weight_ref[...] * strength, axis=0, keepdims=True)
    dpo = jnp.maximum(-margin, 0.0) + jnp.log(1.0 + jnp.exp(-jnp.abs(margin)))
    objective = jnp.sum(kl) + 0.5 * dpo_gamma * jnp.sum(dpo)
    objective_ref[0] = objective
    lines = jnp.concatenate(
        [max_s, 1.0 / sum_s, max_t, 1.0 / sum_t, weight, weight, weight, weight], axis=0
    )
    columns = jnp.transpose(lines)
    max_s, inv_s = columns[:, 0:1], columns[:, 1:2]
    max_t, inv_t, weight = columns[:, 2:3], columns[:, 3:4], columns[:, 4:5]
    target = target_ref[...]
    rows, width = student_ref.shape
    chunk = chunks_ref.shape[2]
    step = 256
    for low in range(0, width, step):
        prob_s = jnp.exp(student_ref[:, low : low + step] - max_s) * inv_s
        prob_t = jnp.exp(teacher_ref[:, low : low + step].astype(f32) - max_t) * inv_t
        column = lax.broadcasted_iota(jnp.int32, (rows, step), 1) + low
        hot = jnp.where(column == target, 1.0, 0.0)
        grad = prob_s - prob_t + weight * (hot - prob_s)
        rounded = grad.astype(bf16)
        grad_ref[:, low : low + step] = rounded
        for j in range(0, step, chunk):
            chunks_ref[(low + j) // chunk] = rounded[:, j : j + chunk]


def make_grad(every, student, teacher, target, into_margin, into_weight, chunks):
    rows, width = student.shape
    f32, bf16 = jnp.float32, jnp.bfloat16
    vmem = pl.BlockSpec(memory_space=pltpu.VMEM)
    return pl.pallas_call(
        grad_kernel,
        out_shape=(
            jax.ShapeDtypeStruct((rows, width), bf16),
            jax.ShapeDtypeStruct((chunks, rows, width // chunks), bf16),
            jax.ShapeDtypeStruct((1,), f32),
        ),
        out_specs=(vmem, vmem, pl.BlockSpec(memory_space=pltpu.SMEM)),
        compiler_params=pltpu.CompilerParams(vmem_limit_bytes=32 * 1024 * 1024),
    )(every, student, teacher, target, into_margin, into_weight)


def head_kernel(core_ref, objective_ref, own_ref, other_ref, grad_ref, out_ref):
    f32, bf16 = jnp.float32, jnp.bfloat16
    grad = grad_ref[...]
    own = jnp.dot(own_ref[...], grad, preferred_element_type=f32).astype(bf16)
    other = jnp.dot(other_ref[...], grad, preferred_element_type=f32).astype(bf16)
    blocks, tall, _ = out_ref.shape
    feats = own.shape[0] // blocks
    extra = tall - 2 * feats
    value = jnp.full((extra, own.shape[1]), objective_ref[0], f32)
    high = value.astype(bf16).astype(f32)
    middle = (value - high).astype(bf16).astype(f32)
    low = value - high - middle
    line = lax.broadcasted_iota(jnp.int32, value.shape, 0)
    pieces = jnp.where(line == 0, high, jnp.where(line == 1, middle, jnp.where(line == 2, low, 0.0)))
    pieces = pieces.astype(bf16)

    def store(first, second):
        for j in range(blocks):
            out_ref[j, :feats] = first[j * feats : (j + 1) * feats]
            out_ref[j, feats : 2 * feats] = second[j * feats : (j + 1) * feats]
            out_ref[j, 2 * feats :] = pieces

    @pl.when(core_ref[0] == 0)
    def _():
        store(own, other)

    @pl.when(core_ref[0] != 0)
    def _():
        store(other, own)


def head_partial(core, objective, own, other, grad, blocks, extra):
    tall, rows = own.shape
    cols = grad.shape[1]
    steps = 4
    per = blocks // steps
    feats = tall // blocks
    return pl.pallas_call(
        head_kernel,
        out_shape=jax.ShapeDtypeStruct((blocks, 2 * feats + extra, cols), jnp.bfloat16),
        grid=(steps,),
        in_specs=[
            pl.BlockSpec(memory_space=pltpu.SMEM),
            pl.BlockSpec(memory_space=pltpu.SMEM),
            pl.BlockSpec((tall // steps, rows), lambda i: (i, 0)),
            pl.BlockSpec((tall // steps, rows), lambda i: (i, 0)),
            pl.BlockSpec((rows, cols), lambda i: (0, 0)),
        ],
        out_specs=pl.BlockSpec((per, 2 * feats + extra, cols), lambda i: (i, 0, 0)),
        compiler_params=pltpu.CompilerParams(vmem_limit_bytes=32 * 1024 * 1024),
        cost_estimate=pl.CostEstimate(
            flops=4 * tall * rows * cols,
            bytes_accessed=4 * tall * rows + 2 * rows * cols + 4 * tall * cols,
            transcendentals=0,
        ),
    )(core, objective, own, other, grad)


def unpack_kernel(parts_ref, grad_ref, total_ref):
    f32 = jnp.float32
    count, _, cols = parts_ref.shape
    tall = grad_ref.shape[0]
    for j in range(count):
        grad_ref[:, j * cols : (j + 1) * cols] = parts_ref[j, :tall].astype(f32)
    lines = jnp.sum(parts_ref[:, tall:].astype(f32), axis=0)
    total_ref[0] = jnp.sum(lines[:3, :1])


def unpack(parts, tall):
    count, _, cols = parts.shape
    return pl.pallas_call(
        unpack_kernel,
        out_shape=(
            jax.ShapeDtypeStruct((tall, count * cols), jnp.float32),
            jax.ShapeDtypeStruct((1,), jnp.float32),
        ),
        out_specs=(pl.BlockSpec(memory_space=pltpu.VMEM), pl.BlockSpec(memory_space=pltpu.SMEM)),
        compiler_params=pltpu.CompilerParams(vmem_limit_bytes=16 * 1024 * 1024),
    )(parts)


def on_device(hidden, head_weight, teacher_logits, target_ids, segment_ids, pair_order):
    f32, bf16 = jnp.float32, jnp.bfloat16
    n_vocab = lax.axis_size("vocab")
    n_dp = lax.axis_size("dp")
    rows, feats = hidden.shape
    width = head_weight.shape[1]
    pairs = n_vocab // 2
    core = lax.axis_index("vocab") % 2
    same_core = [[2 * j + c for j in range(pairs)] for c in range(2)]
    swap = [(i, i ^ 1) for i in range(n_vocab)]
    side = math.isqrt(pairs)
    index = lax.axis_index("vocab")
    place_x, place_y = index // (2 * side), index // 2 % side

    def around(i, along_x, distance):
        x, y, c = i // (2 * side), i // 2 % side, i % 2
        x, y = ((x + distance) % side, y) if along_x else (x, (y + distance) % side)
        return (x * side + y) * 2 + c

    around_x = [[(i, around(i, True, d)) for i in range(n_vocab)] for d in range(side)]
    around_y = [[(i, around(i, False, d)) for i in range(n_vocab)] for d in range(side)]
    weight_full = lax.all_gather(head_weight, "dp", axis=0, tiled=True)
    by_group = to_all(hidden.T, "dp").reshape(n_dp, feats, rows)
    by_pair = to_all(by_group, "vocab", same_core).reshape(pairs, n_dp, feats, rows)
    own_t = relayout(by_pair)
    other_t = lax.ppermute(own_t, "vocab", swap)
    place = lax.axis_index("dp")

    def by_core(own, other, axis):
        return jnp.stack([jnp.where(core == 0, own, other), jnp.where(core == 0, other, own)], axis=axis)

    mine = lax.dynamic_slice_in_dim(own_t, place * rows, rows, 1).reshape(pairs, feats, rows)
    theirs = lax.dynamic_slice_in_dim(other_t, place * rows, rows, 1).reshape(pairs, feats, rows)
    rows_t = by_core(mine, theirs, 1).reshape(n_vocab * feats, rows)
    into_margin, into_weight = pair_signs(segment_ids[0], pair_order[0])
    tn = (((0,), (0,)), ((), ()))
    nt = (((1,), (1,)), ((), ()))
    student = lax.dot_general(rows_t, weight_full, tn, preferred_element_type=f32)
    teacher = teacher_logits.astype(f32)
    offset = lax.axis_index("vocab") * width
    column = lax.broadcasted_iota(jnp.int32, student.shape, 1) + offset
    is_target = column == target_ids[:, None]
    own_max = jnp.max(student, axis=1)
    own_tmax = jnp.max(teacher, axis=1)
    own_exp = jnp.exp(student - own_max[:, None])
    own_texp = jnp.exp(teacher - own_tmax[:, None])
    stats = jnp.stack(
        [
            own_max,
            own_tmax,
            jnp.sum(own_exp, axis=1),
            jnp.sum(own_texp, axis=1),
            jnp.sum(own_texp * (teacher - student), axis=1),
            jnp.sum(jnp.where(is_target, student, 0.0), axis=1),
            jnp.sum(jnp.where(is_target, teacher, 0.0), axis=1),
            jnp.zeros((rows,), f32),
        ]
    )
    every = to_all(stats, "vocab").reshape(n_vocab, 8, rows)
    logit_grad, chunks, objective = make_grad(
        every, student, teacher_logits, (target_ids - offset)[:, None], into_margin, into_weight, n_dp
    )
    chunks = lax.all_to_all(chunks, "dp", 0, 0, tiled=True)
    term = lax.dot_general(weight_full, logit_grad, nt, preferred_element_type=f32).astype(bf16)
    term = term.reshape(side * side, 2, feats, rows)
    kept = lax.dynamic_index_in_dim(term, core, 1, keepdims=False)
    sent = lax.dynamic_index_in_dim(term, 1 - core, 1, keepdims=False)
    term = kept.astype(f32) + lax.ppermute(sent, "vocab", swap).astype(f32)
    term = ring_sum(term.reshape(side, side, feats, rows), place_x, around_x)
    chunks, term = lax.optimization_barrier((chunks, term))
    partial = head_partial(
        core.astype(jnp.int32).reshape(1),
        objective,
        own_t,
        other_t,
        chunks.reshape(n_dp * rows, width // n_dp),
        pairs,
        16,
    )
    partial, term = lax.optimization_barrier((partial, term))
    parts = lax.all_to_all(partial, "dp", 0, 0, tiled=True)
    hidden_grad = ring_sum(term, place_y, around_y).astype(bf16).T
    head_grad, total = unpack(parts, 2 * feats)
    loss_value = total[0] / (rows * n_dp)
    return (hidden_grad, head_grad, loss_value)


def solution(mesh):
    return jax.shard_map(
        on_device,
        mesh=mesh,
        in_specs=(
            P("dp", "vocab"),
            P("dp", "vocab"),
            P("dp", "vocab"),
            P("dp"),
            P("dp", None),
            P("dp", None),
        ),
        out_specs=(P("dp", "vocab"), P("dp", "vocab"), P()),
        check_vma=False,
    )
```

```python
import math

import jax
import jax.numpy as jnp
from jax import lax
from jax.experimental import pallas as pl
from jax.experimental.pallas import tpu as pltpu
from jax.sharding import PartitionSpec as P

dpo_beta = 0.1
dpo_gamma = 4.0


def pair_signs(segments, ordering):
    count = ordering.shape[0]
    labels = lax.broadcasted_iota(jnp.int32, (count, 1), 0)
    seq_hot = (segments[None, :] == labels).astype(jnp.float32)
    chosen = (labels == ordering[None, 0::2]).astype(jnp.float32)
    rejected = (labels == ordering[None, 1::2]).astype(jnp.float32)
    side = chosen - rejected
    pair = chosen + rejected
    margin_sign = jnp.sum(pair[:, None, :] * side[None, :, :], axis=2)
    into_margin = jnp.sum(margin_sign[:, :, None] * seq_hot[None, :, :], axis=1)
    into_weight = jnp.sum(side, axis=1)[:, None] * seq_hot
    return into_margin, into_weight


def to_all(block, axis, groups=None):
    count = lax.axis_size(axis) if groups is None else len(groups[0])
    copies = jnp.broadcast_to(block[None], (count,) + block.shape)
    return lax.all_to_all(copies, axis, 0, 0, axis_index_groups=groups, tiled=True)


def ring_sum(terms, place, around):
    count = terms.shape[0]
    turned = lax.dynamic_slice_in_dim(jnp.concatenate([terms, terms]), place, count, 0)
    rounded = turned.astype(jnp.bfloat16)
    arrived = [lax.ppermute(rounded[d], "vocab", around[d]) for d in range(1, count)]
    return turned[0] + sum(term.astype(jnp.float32) for term in arrived)


def relayout_kernel(in_ref, out_ref):
    groups, _, rows = in_ref.shape[1:]
    for j in range(groups):
        out_ref[:, j * rows : (j + 1) * rows] = in_ref[0, j]


def relayout(by_pair):
    pairs, groups, feats, rows = by_pair.shape
    return pl.pallas_call(
        relayout_kernel,
        out_shape=jax.ShapeDtypeStruct((pairs * feats, groups * rows), by_pair.dtype),
        grid=(pairs,),
        in_specs=[pl.BlockSpec((1, groups, feats, rows), lambda i: (i, 0, 0, 0))],
        out_specs=pl.BlockSpec((feats, groups * rows), lambda i: (i, 0)),
        compiler_params=pltpu.CompilerParams(vmem_limit_bytes=8 * 1024 * 1024),
        cost_estimate=pl.CostEstimate(flops=0, bytes_accessed=4 * by_pair.size, transcendentals=0),
    )(by_pair)


def grad_kernel(
    every_ref, student_ref, teacher_ref, target_ref, margin_ref, weight_ref,
    grad_ref, chunks_ref, objective_ref,
):
    f32, bf16 = jnp.float32, jnp.bfloat16
    maxes_s, maxes_t = every_ref[:, 0, :], every_ref[:, 1, :]
    max_s = jnp.max(maxes_s, axis=0, keepdims=True)
    max_t = jnp.max(maxes_t, axis=0, keepdims=True)
    scale_s = jnp.exp(maxes_s - max_s)
    scale_t = jnp.exp(maxes_t - max_t)
    sum_s = jnp.sum(every_ref[:, 2, :] * scale_s, axis=0, keepdims=True)
    sum_t = jnp.sum(every_ref[:, 3, :] * scale_t, axis=0, keepdims=True)
    cross = jnp.sum(every_ref[:, 4, :] * scale_t, axis=0, keepdims=True)
    target_s = jnp.sum(every_ref[:, 5, :], axis=0, keepdims=True)
    target_t = jnp.sum(every_ref[:, 6, :], axis=0, keepdims=True)
    lse_s = max_s + jnp.log(sum_s)
    lse_t = max_t + jnp.log(sum_t)
    kl = cross / sum_t - lse_t + lse_s
    log_ratio = target_s - lse_s - (target_t - lse_t)
    margin = dpo_beta * jnp.sum(margin_ref[...] * log_ratio, axis=1, keepdims=True)
    strength = dpo_gamma * dpo_beta / (1.0 + jnp.exp(margin))
    weight = -jnp.sum(weight_ref[...] * strength, axis=0, keepdims=True)
    dpo = jnp.maximum(-margin, 0.0) + jnp.log(1.0 + jnp.exp(-jnp.abs(margin)))
    objective = jnp.sum(kl) + 0.5 * dpo_gamma * jnp.sum(dpo)
    objective_ref[0] = objective
    lines = jnp.concatenate(
        [max_s, 1.0 / sum_s, max_t, 1.0 / sum_t, weight, weight, weight, weight], axis=0
    )
    columns = jnp.transpose(lines)
    max_s, inv_s = columns[:, 0:1], columns[:, 1:2]
    max_t, inv_t, weight = columns[:, 2:3], columns[:, 3:4], columns[:, 4:5]
    target = target_ref[...]
    rows, width = student_ref.shape
    chunk = chunks_ref.shape[2]
    step = 256
    for low in range(0, width, step):
        prob_s = jnp.exp(student_ref[:, low : low + step] - max_s) * inv_s
        prob_t = jnp.exp(teacher_ref[:, low : low + step].astype(f32) - max_t) * inv_t
        column = lax.broadcasted_iota(jnp.int32, (rows, step), 1) + low
        hot = jnp.where(column == target, 1.0, 0.0)
        grad = prob_s - prob_t + weight * (hot - prob_s)
        rounded = grad.astype(bf16)
        grad_ref[:, low : low + step] = rounded
        for j in range(0, step, chunk):
            chunks_ref[(low + j) // chunk] = rounded[:, j : j + chunk]


def make_grad(every, student, teacher, target, into_margin, into_weight, chunks):
    rows, width = student.shape
    f32, bf16 = jnp.float32, jnp.bfloat16
    vmem = pl.BlockSpec(memory_space=pltpu.VMEM)
    return pl.pallas_call(
        grad_kernel,
        out_shape=(
            jax.ShapeDtypeStruct((rows, width), bf16),
            jax.ShapeDtypeStruct((chunks, rows, width // chunks), bf16),
            jax.ShapeDtypeStruct((1,), f32),
        ),
        out_specs=(vmem, vmem, pl.BlockSpec(memory_space=pltpu.SMEM)),
        compiler_params=pltpu.CompilerParams(vmem_limit_bytes=12 * 1024 * 1024),
    )(every, student, teacher, target, into_margin, into_weight)


def head_kernel(core_ref, objective_ref, own_ref, other_ref, grad_ref, out_ref):
    f32, bf16 = jnp.float32, jnp.bfloat16
    grad = grad_ref[...]
    own = jnp.dot(own_ref[...], grad, preferred_element_type=f32).astype(bf16)
    other = jnp.dot(other_ref[...], grad, preferred_element_type=f32).astype(bf16)
    blocks, tall, _ = out_ref.shape
    feats = own.shape[0] // blocks
    extra = tall - 2 * feats
    value = jnp.full((extra, own.shape[1]), objective_ref[0], f32)
    high = value.astype(bf16).astype(f32)
    middle = (value - high).astype(bf16).astype(f32)
    low = value - high - middle
    line = lax.broadcasted_iota(jnp.int32, value.shape, 0)
    pieces = jnp.where(line == 0, high, jnp.where(line == 1, middle, jnp.where(line == 2, low, 0.0)))
    pieces = pieces.astype(bf16)

    def store(first, second):
        for j in range(blocks):
            out_ref[j, :feats] = first[j * feats : (j + 1) * feats]
            out_ref[j, feats : 2 * feats] = second[j * feats : (j + 1) * feats]
            out_ref[j, 2 * feats :] = pieces

    @pl.when(core_ref[0] == 0)
    def _():
        store(own, other)

    @pl.when(core_ref[0] != 0)
    def _():
        store(other, own)


def head_partial(core, objective, own, other, grad, blocks, extra):
    tall, rows = own.shape
    cols = grad.shape[1]
    steps = 8
    per = blocks // steps
    feats = tall // blocks
    return pl.pallas_call(
        head_kernel,
        out_shape=jax.ShapeDtypeStruct((blocks, 2 * feats + extra, cols), jnp.bfloat16),
        grid=(steps,),
        in_specs=[
            pl.BlockSpec(memory_space=pltpu.SMEM),
            pl.BlockSpec(memory_space=pltpu.SMEM),
            pl.BlockSpec((tall // steps, rows), lambda i: (i, 0)),
            pl.BlockSpec((tall // steps, rows), lambda i: (i, 0)),
            pl.BlockSpec((rows, cols), lambda i: (0, 0)),
        ],
        out_specs=pl.BlockSpec((per, 2 * feats + extra, cols), lambda i: (i, 0, 0)),
        compiler_params=pltpu.CompilerParams(vmem_limit_bytes=8 * 1024 * 1024),
        cost_estimate=pl.CostEstimate(
            flops=4 * tall * rows * cols,
            bytes_accessed=4 * tall * rows + 2 * rows * cols + 4 * tall * cols,
            transcendentals=0,
        ),
    )(core, objective, own, other, grad)


def unpack_kernel(parts_ref, grad_ref, total_ref):
    f32 = jnp.float32
    count, _, cols = parts_ref.shape
    tall = grad_ref.shape[0]
    for j in range(count):
        grad_ref[:, j * cols : (j + 1) * cols] = parts_ref[j, :tall].astype(f32)
    lines = jnp.sum(parts_ref[:, tall:].astype(f32), axis=0)
    total_ref[0] = jnp.sum(lines[:3, :1])


def unpack(parts, tall):
    count, _, cols = parts.shape
    return pl.pallas_call(
        unpack_kernel,
        out_shape=(
            jax.ShapeDtypeStruct((tall, count * cols), jnp.float32),
            jax.ShapeDtypeStruct((1,), jnp.float32),
        ),
        out_specs=(pl.BlockSpec(memory_space=pltpu.VMEM), pl.BlockSpec(memory_space=pltpu.SMEM)),
        compiler_params=pltpu.CompilerParams(vmem_limit_bytes=8 * 1024 * 1024),
    )(parts)


def on_device(hidden, head_weight, teacher_logits, target_ids, segment_ids, pair_order):
    f32, bf16 = jnp.float32, jnp.bfloat16
    n_vocab = lax.axis_size("vocab")
    n_dp = lax.axis_size("dp")
    rows, feats = hidden.shape
    width = head_weight.shape[1]
    pairs = n_vocab // 2
    core = lax.axis_index("vocab") % 2
    same_core = [[2 * j + c for j in range(pairs)] for c in range(2)]
    swap = [(i, i ^ 1) for i in range(n_vocab)]
    side = math.isqrt(pairs)
    index = lax.axis_index("vocab")
    place_x, place_y = index // (2 * side), index // 2 % side

    def around(i, along_x, distance):
        x, y, c = i // (2 * side), i // 2 % side, i % 2
        x, y = ((x + distance) % side, y) if along_x else (x, (y + distance) % side)
        return (x * side + y) * 2 + c

    around_x = [[(i, around(i, True, d)) for i in range(n_vocab)] for d in range(side)]
    around_y = [[(i, around(i, False, d)) for i in range(n_vocab)] for d in range(side)]
    weight_full = lax.all_gather(head_weight, "dp", axis=0, tiled=True)
    by_group = lax.all_gather(hidden.T, "dp")
    by_pair = to_all(by_group, "vocab", same_core).reshape(pairs, n_dp, feats, rows)
    own_t = relayout(by_pair)
    other_t = lax.ppermute(own_t, "vocab", swap)
    place = lax.axis_index("dp")

    def by_core(own, other, axis):
        return jnp.stack([jnp.where(core == 0, own, other), jnp.where(core == 0, other, own)], axis=axis)

    mine = lax.dynamic_slice_in_dim(own_t, place * rows, rows, 1).reshape(pairs, feats, rows)
    theirs = lax.dynamic_slice_in_dim(other_t, place * rows, rows, 1).reshape(pairs, feats, rows)
    rows_t = by_core(mine, theirs, 1).reshape(n_vocab * feats, rows)
    into_margin, into_weight = pair_signs(segment_ids[0], pair_order[0])
    tn = (((0,), (0,)), ((), ()))
    nt = (((1,), (1,)), ((), ()))
    student = lax.dot_general(rows_t, weight_full, tn, preferred_element_type=f32)
    teacher = teacher_logits.astype(f32)
    offset = lax.axis_index("vocab") * width
    column = lax.broadcasted_iota(jnp.int32, student.shape, 1) + offset
    is_target = column == target_ids[:, None]
    own_max = jnp.max(student, axis=1)
    own_tmax = jnp.max(teacher, axis=1)
    own_exp = jnp.exp(student - own_max[:, None])
    own_texp = jnp.exp(teacher - own_tmax[:, None])
    stats = jnp.stack(
        [
            own_max,
            own_tmax,
            jnp.sum(own_exp, axis=1),
            jnp.sum(own_texp, axis=1),
            jnp.sum(own_texp * (teacher - student), axis=1),
            jnp.sum(jnp.where(is_target, student, 0.0), axis=1),
            jnp.sum(jnp.where(is_target, teacher, 0.0), axis=1),
            jnp.zeros((rows,), f32),
        ]
    )
    every = to_all(stats, "vocab").reshape(n_vocab, 8, rows)
    logit_grad, chunks, objective = make_grad(
        every, student, teacher_logits, (target_ids - offset)[:, None], into_margin, into_weight, n_dp
    )
    chunks = lax.all_to_all(chunks, "dp", 0, 0, tiled=True)
    term = lax.dot_general(weight_full, logit_grad, nt, preferred_element_type=f32).astype(bf16)
    term = term.reshape(side * side, 2, feats, rows)
    kept = lax.dynamic_index_in_dim(term, core, 1, keepdims=False)
    sent = lax.dynamic_index_in_dim(term, 1 - core, 1, keepdims=False)
    term = kept.astype(f32) + lax.ppermute(sent, "vocab", swap).astype(f32)
    term = ring_sum(term.reshape(side, side, feats, rows), place_x, around_x)
    chunks, term = lax.optimization_barrier((chunks, term))
    partial = head_partial(
        core.astype(jnp.int32).reshape(1),
        objective,
        own_t,
        other_t,
        chunks.reshape(n_dp * rows, width // n_dp),
        pairs,
        16,
    )
    partial, term = lax.optimization_barrier((partial, term))
    parts = lax.all_to_all(partial, "dp", 0, 0, tiled=True)
    hidden_grad = ring_sum(term, place_y, around_y).astype(bf16).T
    head_grad, total = unpack(parts, 2 * feats)
    loss_value = total[0] / (rows * n_dp)
    return (hidden_grad, head_grad, loss_value)


def solution(mesh):
    return jax.shard_map(
        on_device,
        mesh=mesh,
        in_specs=(
            P("dp", "vocab"),
            P("dp", "vocab"),
            P("dp", "vocab"),
            P("dp"),
            P("dp", None),
            P("dp", None),
        ),
        out_specs=(P("dp", "vocab"), P("dp", "vocab"), P()),
        check_vma=False,
    )
```

```python
import math

import jax
import jax.numpy as jnp
from jax import lax
from jax.experimental import pallas as pl
from jax.experimental.pallas import tpu as pltpu
from jax.sharding import PartitionSpec as P

dpo_beta = 0.1
dpo_gamma = 4.0


def pair_signs(segments, ordering):
    count = ordering.shape[0]
    labels = lax.broadcasted_iota(jnp.int32, (count, 1), 0)
    seq_hot = (segments[None, :] == labels).astype(jnp.float32)
    chosen = (labels == ordering[None, 0::2]).astype(jnp.float32)
    rejected = (labels == ordering[None, 1::2]).astype(jnp.float32)
    side = chosen - rejected
    pair = chosen + rejected
    margin_sign = jnp.sum(pair[:, None, :] * side[None, :, :], axis=2)
    into_margin = jnp.sum(margin_sign[:, :, None] * seq_hot[None, :, :], axis=1)
    into_weight = jnp.sum(side, axis=1)[:, None] * seq_hot
    return into_margin, into_weight


def to_all(block, axis, groups=None):
    count = lax.axis_size(axis) if groups is None else len(groups[0])
    copies = jnp.broadcast_to(block[None], (count,) + block.shape)
    return lax.all_to_all(copies, axis, 0, 0, axis_index_groups=groups, tiled=True)


def ring_sum(terms, place, around):
    count = terms.shape[0]
    turned = lax.dynamic_slice_in_dim(jnp.concatenate([terms, terms]), place, count, 0)
    rounded = turned.astype(jnp.bfloat16)
    arrived = [lax.ppermute(rounded[d], "vocab", around[d]) for d in range(1, count)]
    return turned[0] + sum(term.astype(jnp.float32) for term in arrived)


def relayout_kernel(in_ref, out_ref):
    groups, _, rows = in_ref.shape[1:]
    for j in range(groups):
        out_ref[:, j * rows : (j + 1) * rows] = in_ref[0, j]


def relayout(by_pair):
    pairs, groups, feats, rows = by_pair.shape
    return pl.pallas_call(
        relayout_kernel,
        out_shape=jax.ShapeDtypeStruct((pairs * feats, groups * rows), by_pair.dtype),
        grid=(pairs,),
        in_specs=[pl.BlockSpec((1, groups, feats, rows), lambda i: (i, 0, 0, 0))],
        out_specs=pl.BlockSpec((feats, groups * rows), lambda i: (i, 0)),
        compiler_params=pltpu.CompilerParams(vmem_limit_bytes=8 * 1024 * 1024),
        cost_estimate=pl.CostEstimate(flops=0, bytes_accessed=4 * by_pair.size, transcendentals=0),
    )(by_pair)


def grad_kernel(
    every_ref, student_ref, teacher_ref, target_ref, margin_ref, weight_ref,
    grad_ref, chunks_ref, objective_ref,
):
    f32, bf16 = jnp.float32, jnp.bfloat16
    maxes_s, maxes_t = every_ref[:, 0, :], every_ref[:, 1, :]
    max_s = jnp.max(maxes_s, axis=0, keepdims=True)
    max_t = jnp.max(maxes_t, axis=0, keepdims=True)
    scale_s = jnp.exp(maxes_s - max_s)
    scale_t = jnp.exp(maxes_t - max_t)
    sum_s = jnp.sum(every_ref[:, 2, :] * scale_s, axis=0, keepdims=True)
    sum_t = jnp.sum(every_ref[:, 3, :] * scale_t, axis=0, keepdims=True)
    cross = jnp.sum(every_ref[:, 4, :] * scale_t, axis=0, keepdims=True)
    target_s = jnp.sum(every_ref[:, 5, :], axis=0, keepdims=True)
    target_t = jnp.sum(every_ref[:, 6, :], axis=0, keepdims=True)
    lse_s = max_s + jnp.log(sum_s)
    lse_t = max_t + jnp.log(sum_t)
    kl = cross / sum_t - lse_t + lse_s
    log_ratio = target_s - lse_s - (target_t - lse_t)
    margin = dpo_beta * jnp.sum(margin_ref[...] * log_ratio, axis=1, keepdims=True)
    strength = dpo_gamma * dpo_beta / (1.0 + jnp.exp(margin))
    weight = -jnp.sum(weight_ref[...] * strength, axis=0, keepdims=True)
    dpo = jnp.maximum(-margin, 0.0) + jnp.log(1.0 + jnp.exp(-jnp.abs(margin)))
    objective = jnp.sum(kl) + 0.5 * dpo_gamma * jnp.sum(dpo)
    objective_ref[0] = objective
    lines = jnp.concatenate(
        [max_s, 1.0 / sum_s, max_t, 1.0 / sum_t, weight, weight, weight, weight], axis=0
    )
    columns = jnp.transpose(lines)
    max_s, inv_s = columns[:, 0:1], columns[:, 1:2]
    max_t, inv_t, weight = columns[:, 2:3], columns[:, 3:4], columns[:, 4:5]
    target = target_ref[...]
    rows, width = student_ref.shape
    chunk = chunks_ref.shape[2]
    step = 256
    for low in range(0, width, step):
        prob_s = jnp.exp(student_ref[:, low : low + step] - max_s) * inv_s
        prob_t = jnp.exp(teacher_ref[:, low : low + step].astype(f32) - max_t) * inv_t
        column = lax.broadcasted_iota(jnp.int32, (rows, step), 1) + low
        hot = jnp.where(column == target, 1.0, 0.0)
        grad = prob_s - prob_t + weight * (hot - prob_s)
        rounded = grad.astype(bf16)
        grad_ref[:, low : low + step] = rounded
        for j in range(0, step, chunk):
            chunks_ref[(low + j) // chunk] = rounded[:, j : j + chunk]


def make_grad(every, student, teacher, target, into_margin, into_weight, chunks):
    rows, width = student.shape
    f32, bf16 = jnp.float32, jnp.bfloat16
    vmem = pl.BlockSpec(memory_space=pltpu.VMEM)
    return pl.pallas_call(
        grad_kernel,
        out_shape=(
            jax.ShapeDtypeStruct((rows, width), bf16),
            jax.ShapeDtypeStruct((chunks, rows, width // chunks), bf16),
            jax.ShapeDtypeStruct((1,), f32),
        ),
        out_specs=(vmem, vmem, pl.BlockSpec(memory_space=pltpu.SMEM)),
        compiler_params=pltpu.CompilerParams(vmem_limit_bytes=12 * 1024 * 1024),
    )(every, student, teacher, target, into_margin, into_weight)


head_steps = 4


def head_kernel(
    core_ref, objective_ref, own_hbm, other_hbm, grad_ref, out_ref,
    own_ref, other_ref, own_sem, other_sem,
):
    f32, bf16 = jnp.float32, jnp.bfloat16
    total, tall, cols = out_ref.shape
    blocks = total // head_steps
    step = own_ref.shape[0] // head_steps
    feats = step // blocks

    def copies(i):
        part = pl.ds(i * step, step)
        return (
            pltpu.make_async_copy(own_hbm.at[part], own_ref.at[part], own_sem.at[i]),
            pltpu.make_async_copy(other_hbm.at[part], other_ref.at[part], other_sem.at[i]),
        )

    for i in range(head_steps):
        for copy in copies(i):
            copy.start()
    value = jnp.full((tall - 2 * feats, cols), objective_ref[0], f32)
    high = value.astype(bf16).astype(f32)
    middle = (value - high).astype(bf16).astype(f32)
    low = value - high - middle
    line = lax.broadcasted_iota(jnp.int32, value.shape, 0)
    pieces = jnp.where(line == 0, high, jnp.where(line == 1, middle, jnp.where(line == 2, low, 0.0)))
    pieces = pieces.astype(bf16)
    for j in range(total):
        out_ref[j, 2 * feats :] = pieces
    for i in range(head_steps):
        for copy in copies(i):
            copy.wait()
        part = slice(i * step, (i + 1) * step)
        own = jnp.dot(own_ref[part], grad_ref[...], preferred_element_type=f32).astype(bf16)
        other = jnp.dot(other_ref[part], grad_ref[...], preferred_element_type=f32).astype(bf16)

        def store(first, second):
            for j in range(blocks):
                out_ref[i * blocks + j, :feats] = first[j * feats : (j + 1) * feats]
                out_ref[i * blocks + j, feats : 2 * feats] = second[j * feats : (j + 1) * feats]

        @pl.when(core_ref[0] == 0)
        def _():
            store(own, other)

        @pl.when(core_ref[0] != 0)
        def _():
            store(other, own)


def head_partial(core, objective, own, other, grad, blocks, extra):
    tall, rows = own.shape
    cols = grad.shape[1]
    feats = tall // blocks
    smem = pl.BlockSpec(memory_space=pltpu.SMEM)
    vmem = pl.BlockSpec(memory_space=pltpu.VMEM)
    hbm = pl.BlockSpec(memory_space=pl.ANY)
    return pl.pallas_call(
        head_kernel,
        out_shape=jax.ShapeDtypeStruct((blocks, 2 * feats + extra, cols), jnp.bfloat16),
        in_specs=[smem, smem, hbm, hbm, vmem],
        out_specs=vmem,
        scratch_shapes=[
            pltpu.VMEM((tall, rows), own.dtype),
            pltpu.VMEM((tall, rows), own.dtype),
            pltpu.SemaphoreType.DMA((head_steps,)),
            pltpu.SemaphoreType.DMA((head_steps,)),
        ],
        compiler_params=pltpu.CompilerParams(vmem_limit_bytes=32 * 1024 * 1024),
        cost_estimate=pl.CostEstimate(
            flops=4 * tall * rows * cols,
            bytes_accessed=4 * tall * rows + 2 * rows * cols + 4 * tall * cols,
            transcendentals=0,
        ),
    )(core, objective, own, other, grad)


def unpack_kernel(parts_ref, grad_ref, total_ref):
    f32 = jnp.float32
    count, _, cols = parts_ref.shape
    tall = grad_ref.shape[0]
    for j in range(count):
        grad_ref[:, j * cols : (j + 1) * cols] = parts_ref[j, :tall].astype(f32)
    lines = jnp.sum(parts_ref[:, tall:].astype(f32), axis=0)
    total_ref[0] = jnp.sum(lines[:3, :1])


def unpack(parts, tall):
    count, _, cols = parts.shape
    return pl.pallas_call(
        unpack_kernel,
        out_shape=(
            jax.ShapeDtypeStruct((tall, count * cols), jnp.float32),
            jax.ShapeDtypeStruct((1,), jnp.float32),
        ),
        out_specs=(pl.BlockSpec(memory_space=pltpu.VMEM), pl.BlockSpec(memory_space=pltpu.SMEM)),
        compiler_params=pltpu.CompilerParams(vmem_limit_bytes=8 * 1024 * 1024),
    )(parts)


def on_device(hidden, head_weight, teacher_logits, target_ids, segment_ids, pair_order):
    f32, bf16 = jnp.float32, jnp.bfloat16
    n_vocab = lax.axis_size("vocab")
    n_dp = lax.axis_size("dp")
    rows, feats = hidden.shape
    width = head_weight.shape[1]
    pairs = n_vocab // 2
    core = lax.axis_index("vocab") % 2
    same_core = [[2 * j + c for j in range(pairs)] for c in range(2)]
    swap = [(i, i ^ 1) for i in range(n_vocab)]
    side = math.isqrt(pairs)
    index = lax.axis_index("vocab")
    place_x, place_y = index // (2 * side), index // 2 % side

    def around(i, along_x, distance):
        x, y, c = i // (2 * side), i // 2 % side, i % 2
        x, y = ((x + distance) % side, y) if along_x else (x, (y + distance) % side)
        return (x * side + y) * 2 + c

    around_x = [[(i, around(i, True, d)) for i in range(n_vocab)] for d in range(side)]
    around_y = [[(i, around(i, False, d)) for i in range(n_vocab)] for d in range(side)]
    weight_full = lax.all_gather(head_weight, "dp", axis=0, tiled=True)
    by_group = lax.all_gather(hidden.T, "dp")
    by_pair = to_all(by_group, "vocab", same_core).reshape(pairs, n_dp, feats, rows)
    own_t = relayout(by_pair)
    other_t = lax.ppermute(own_t, "vocab", swap)
    place = lax.axis_index("dp")

    def by_core(own, other, axis):
        return jnp.stack([jnp.where(core == 0, own, other), jnp.where(core == 0, other, own)], axis=axis)

    mine = lax.dynamic_slice_in_dim(own_t, place * rows, rows, 1).reshape(pairs, feats, rows)
    theirs = lax.dynamic_slice_in_dim(other_t, place * rows, rows, 1).reshape(pairs, feats, rows)
    rows_t = by_core(mine, theirs, 1).reshape(n_vocab * feats, rows)
    into_margin, into_weight = pair_signs(segment_ids[0], pair_order[0])
    tn = (((0,), (0,)), ((), ()))
    nt = (((1,), (1,)), ((), ()))
    student = lax.dot_general(rows_t, weight_full, tn, preferred_element_type=f32)
    teacher = teacher_logits.astype(f32)
    offset = lax.axis_index("vocab") * width
    column = lax.broadcasted_iota(jnp.int32, student.shape, 1) + offset
    is_target = column == target_ids[:, None]
    own_max = jnp.max(student, axis=1)
    own_tmax = jnp.max(teacher, axis=1)
    own_exp = jnp.exp(student - own_max[:, None])
    own_texp = jnp.exp(teacher - own_tmax[:, None])
    stats = jnp.stack(
        [
            own_max,
            own_tmax,
            jnp.sum(own_exp, axis=1),
            jnp.sum(own_texp, axis=1),
            jnp.sum(own_texp * (teacher - student), axis=1),
            jnp.sum(jnp.where(is_target, student, 0.0), axis=1),
            jnp.sum(jnp.where(is_target, teacher, 0.0), axis=1),
            jnp.zeros((rows,), f32),
        ]
    )
    every = to_all(stats, "vocab").reshape(n_vocab, 8, rows)
    logit_grad, chunks, objective = make_grad(
        every, student, teacher_logits, (target_ids - offset)[:, None], into_margin, into_weight, n_dp
    )
    chunks = lax.all_to_all(chunks, "dp", 0, 0, tiled=True)
    term = lax.dot_general(weight_full, logit_grad, nt, preferred_element_type=f32).astype(bf16)
    term = term.reshape(side * side, 2, feats, rows)
    kept = lax.dynamic_index_in_dim(term, core, 1, keepdims=False)
    sent = lax.dynamic_index_in_dim(term, 1 - core, 1, keepdims=False)
    term = kept.astype(f32) + lax.ppermute(sent, "vocab", swap).astype(f32)
    term = ring_sum(term.reshape(side, side, feats, rows), place_x, around_x)
    chunks, term = lax.optimization_barrier((chunks, term))
    partial = head_partial(
        core.astype(jnp.int32).reshape(1),
        objective,
        own_t,
        other_t,
        chunks.reshape(n_dp * rows, width // n_dp),
        pairs,
        16,
    )
    partial, term = lax.optimization_barrier((partial, term))
    parts = lax.all_to_all(partial, "dp", 0, 0, tiled=True)
    hidden_grad = ring_sum(term, place_y, around_y).astype(bf16).T
    head_grad, total = unpack(parts, 2 * feats)
    loss_value = total[0] / (rows * n_dp)
    return (hidden_grad, head_grad, loss_value)


def solution(mesh):
    return jax.shard_map(
        on_device,
        mesh=mesh,
        in_specs=(
            P("dp", "vocab"),
            P("dp", "vocab"),
            P("dp", "vocab"),
            P("dp"),
            P("dp", None),
            P("dp", None),
        ),
        out_specs=(P("dp", "vocab"), P("dp", "vocab"), P()),
        check_vma=False,
    )
```

```python
import math

import jax
import jax.numpy as jnp
from jax import lax
from jax.experimental import pallas as pl
from jax.experimental.pallas import tpu as pltpu
from jax.sharding import PartitionSpec as P

dpo_beta = 0.1
dpo_gamma = 4.0


def pair_signs(segments, ordering):
    count = ordering.shape[0]
    labels = lax.broadcasted_iota(jnp.int32, (count, 1), 0)
    seq_hot = (segments[None, :] == labels).astype(jnp.float32)
    chosen = (labels == ordering[None, 0::2]).astype(jnp.float32)
    rejected = (labels == ordering[None, 1::2]).astype(jnp.float32)
    side = chosen - rejected
    pair = chosen + rejected
    margin_sign = jnp.sum(pair[:, None, :] * side[None, :, :], axis=2)
    into_margin = jnp.sum(margin_sign[:, :, None] * seq_hot[None, :, :], axis=1)
    into_weight = jnp.sum(side, axis=1)[:, None] * seq_hot
    return into_margin, into_weight


def to_all(block, axis, groups=None):
    count = lax.axis_size(axis) if groups is None else len(groups[0])
    copies = jnp.broadcast_to(block[None], (count,) + block.shape)
    return lax.all_to_all(copies, axis, 0, 0, axis_index_groups=groups, tiled=True)


def ring_sum(terms, place, around):
    count = terms.shape[0]
    turned = lax.dynamic_slice_in_dim(jnp.concatenate([terms, terms]), place, count, 0)
    rounded = turned.astype(jnp.bfloat16)
    arrived = [lax.ppermute(rounded[d], "vocab", around[d]) for d in range(1, count)]
    return turned[0] + sum(term.astype(jnp.float32) for term in arrived)


def relayout_kernel(in_ref, out_ref):
    groups, _, rows = in_ref.shape[1:]
    for j in range(groups):
        out_ref[:, j * rows : (j + 1) * rows] = in_ref[0, j]


def relayout(by_pair):
    pairs, groups, feats, rows = by_pair.shape
    return pl.pallas_call(
        relayout_kernel,
        out_shape=jax.ShapeDtypeStruct((pairs * feats, groups * rows), by_pair.dtype),
        grid=(pairs,),
        in_specs=[pl.BlockSpec((1, groups, feats, rows), lambda i: (i, 0, 0, 0))],
        out_specs=pl.BlockSpec((feats, groups * rows), lambda i: (i, 0)),
        compiler_params=pltpu.CompilerParams(vmem_limit_bytes=8 * 1024 * 1024),
        cost_estimate=pl.CostEstimate(flops=0, bytes_accessed=4 * by_pair.size, transcendentals=0),
    )(by_pair)


def stats_kernel(student_ref, teacher_ref, target_ref, out_ref):
    f32 = jnp.float32
    rows, width = student_ref.shape
    step = 256
    lows = range(0, width, step)
    max_s = student_ref[:, :step]
    max_t = teacher_ref[:, :step].astype(f32)
    for low in lows[1:]:
        max_s = jnp.maximum(max_s, student_ref[:, low : low + step])
        max_t = jnp.maximum(max_t, teacher_ref[:, low : low + step].astype(f32))
    max_s = jnp.max(max_s, axis=1, keepdims=True)
    max_t = jnp.max(max_t, axis=1, keepdims=True)
    target = target_ref[...]
    zero = jnp.zeros((rows, step), f32)
    sum_s, sum_t, cross, target_s, target_t = zero, zero, zero, zero, zero
    for low in lows:
        student = student_ref[:, low : low + step]
        teacher = teacher_ref[:, low : low + step].astype(f32)
        weight = jnp.exp(teacher - max_t)
        sum_s += jnp.exp(student - max_s)
        sum_t += weight
        cross += weight * (teacher - student)
        hot = lax.broadcasted_iota(jnp.int32, (rows, step), 1) + low == target
        target_s += jnp.where(hot, student, 0.0)
        target_t += jnp.where(hot, teacher, 0.0)
    sums = [jnp.sum(x, axis=1, keepdims=True) for x in (sum_s, sum_t, cross, target_s, target_t)]
    lines = jnp.transpose(jnp.concatenate([max_s, max_t] + sums + [max_s], axis=1))
    for i in range(out_ref.shape[0]):
        out_ref[i] = lines


def local_stats(student, teacher, target, copies):
    return pl.pallas_call(
        stats_kernel,
        out_shape=jax.ShapeDtypeStruct((copies, 8, student.shape[0]), jnp.float32),
        compiler_params=pltpu.CompilerParams(vmem_limit_bytes=12 * 1024 * 1024),
    )(student, teacher, target)


def grad_kernel(
    every_ref, student_ref, teacher_ref, target_ref, margin_ref, weight_ref,
    grad_ref, chunks_ref, objective_ref,
):
    f32, bf16 = jnp.float32, jnp.bfloat16
    maxes_s, maxes_t = every_ref[:, 0, :], every_ref[:, 1, :]
    max_s = jnp.max(maxes_s, axis=0, keepdims=True)
    max_t = jnp.max(maxes_t, axis=0, keepdims=True)
    scale_s = jnp.exp(maxes_s - max_s)
    scale_t = jnp.exp(maxes_t - max_t)
    sum_s = jnp.sum(every_ref[:, 2, :] * scale_s, axis=0, keepdims=True)
    sum_t = jnp.sum(every_ref[:, 3, :] * scale_t, axis=0, keepdims=True)
    cross = jnp.sum(every_ref[:, 4, :] * scale_t, axis=0, keepdims=True)
    target_s = jnp.sum(every_ref[:, 5, :], axis=0, keepdims=True)
    target_t = jnp.sum(every_ref[:, 6, :], axis=0, keepdims=True)
    lse_s = max_s + jnp.log(sum_s)
    lse_t = max_t + jnp.log(sum_t)
    kl = cross / sum_t - lse_t + lse_s
    log_ratio = target_s - lse_s - (target_t - lse_t)
    margin = dpo_beta * jnp.sum(margin_ref[...] * log_ratio, axis=1, keepdims=True)
    strength = dpo_gamma * dpo_beta / (1.0 + jnp.exp(margin))
    weight = -jnp.sum(weight_ref[...] * strength, axis=0, keepdims=True)
    dpo = jnp.maximum(-margin, 0.0) + jnp.log(1.0 + jnp.exp(-jnp.abs(margin)))
    objective = jnp.sum(kl) + 0.5 * dpo_gamma * jnp.sum(dpo)
    objective_ref[0] = objective
    lines = jnp.concatenate(
        [max_s, 1.0 / sum_s, max_t, 1.0 / sum_t, weight, weight, weight, weight], axis=0
    )
    columns = jnp.transpose(lines)
    max_s, inv_s = columns[:, 0:1], columns[:, 1:2]
    max_t, inv_t, weight = columns[:, 2:3], columns[:, 3:4], columns[:, 4:5]
    target = target_ref[...]
    rows, width = student_ref.shape
    chunk = chunks_ref.shape[2]
    step = 256
    for low in range(0, width, step):
        prob_s = jnp.exp(student_ref[:, low : low + step] - max_s) * inv_s
        prob_t = jnp.exp(teacher_ref[:, low : low + step].astype(f32) - max_t) * inv_t
        column = lax.broadcasted_iota(jnp.int32, (rows, step), 1) + low
        hot = jnp.where(column == target, 1.0, 0.0)
        grad = prob_s - prob_t + weight * (hot - prob_s)
        rounded = grad.astype(bf16)
        grad_ref[:, low : low + step] = rounded
        for j in range(0, step, chunk):
            chunks_ref[(low + j) // chunk] = rounded[:, j : j + chunk]


def make_grad(every, student, teacher, target, into_margin, into_weight, chunks):
    rows, width = student.shape
    f32, bf16 = jnp.float32, jnp.bfloat16
    vmem = pl.BlockSpec(memory_space=pltpu.VMEM)
    return pl.pallas_call(
        grad_kernel,
        out_shape=(
            jax.ShapeDtypeStruct((rows, width), bf16),
            jax.ShapeDtypeStruct((chunks, rows, width // chunks), bf16),
            jax.ShapeDtypeStruct((1,), f32),
        ),
        out_specs=(vmem, vmem, pl.BlockSpec(memory_space=pltpu.SMEM)),
        compiler_params=pltpu.CompilerParams(vmem_limit_bytes=12 * 1024 * 1024),
    )(every, student, teacher, target, into_margin, into_weight)


head_steps = 4


def head_kernel(
    core_ref, objective_ref, own_hbm, other_hbm, grad_ref, out_ref,
    own_ref, other_ref, own_sem, other_sem,
):
    f32, bf16 = jnp.float32, jnp.bfloat16
    total, tall, cols = out_ref.shape
    blocks = total // head_steps
    step = own_ref.shape[0] // head_steps
    feats = step // blocks

    def copies(i):
        part = pl.ds(i * step, step)
        return (
            pltpu.make_async_copy(own_hbm.at[part], own_ref.at[part], own_sem.at[i]),
            pltpu.make_async_copy(other_hbm.at[part], other_ref.at[part], other_sem.at[i]),
        )

    for i in range(head_steps):
        for copy in copies(i):
            copy.start()
    value = jnp.full((tall - 2 * feats, cols), objective_ref[0], f32)
    high = value.astype(bf16).astype(f32)
    middle = (value - high).astype(bf16).astype(f32)
    low = value - high - middle
    line = lax.broadcasted_iota(jnp.int32, value.shape, 0)
    pieces = jnp.where(line == 0, high, jnp.where(line == 1, middle, jnp.where(line == 2, low, 0.0)))
    pieces = pieces.astype(bf16)
    for j in range(total):
        out_ref[j, 2 * feats :] = pieces
    for i in range(head_steps):
        for copy in copies(i):
            copy.wait()
        part = slice(i * step, (i + 1) * step)
        own = jnp.dot(own_ref[part], grad_ref[...], preferred_element_type=f32).astype(bf16)
        other = jnp.dot(other_ref[part], grad_ref[...], preferred_element_type=f32).astype(bf16)

        def store(first, second):
            for j in range(blocks):
                out_ref[i * blocks + j, :feats] = first[j * feats : (j + 1) * feats]
                out_ref[i * blocks + j, feats : 2 * feats] = second[j * feats : (j + 1) * feats]

        @pl.when(core_ref[0] == 0)
        def _():
            store(own, other)

        @pl.when(core_ref[0] != 0)
        def _():
            store(other, own)


def head_partial(core, objective, own, other, grad, blocks, extra):
    tall, rows = own.shape
    cols = grad.shape[1]
    feats = tall // blocks
    smem = pl.BlockSpec(memory_space=pltpu.SMEM)
    vmem = pl.BlockSpec(memory_space=pltpu.VMEM)
    hbm = pl.BlockSpec(memory_space=pl.ANY)
    return pl.pallas_call(
        head_kernel,
        out_shape=jax.ShapeDtypeStruct((blocks, 2 * feats + extra, cols), jnp.bfloat16),
        in_specs=[smem, smem, hbm, hbm, vmem],
        out_specs=vmem,
        scratch_shapes=[
            pltpu.VMEM((tall, rows), own.dtype),
            pltpu.VMEM((tall, rows), own.dtype),
            pltpu.SemaphoreType.DMA((head_steps,)),
            pltpu.SemaphoreType.DMA((head_steps,)),
        ],
        compiler_params=pltpu.CompilerParams(vmem_limit_bytes=32 * 1024 * 1024),
        cost_estimate=pl.CostEstimate(
            flops=4 * tall * rows * cols,
            bytes_accessed=4 * tall * rows + 2 * rows * cols + 4 * tall * cols,
            transcendentals=0,
        ),
    )(core, objective, own, other, grad)


def unpack_kernel(parts_ref, grad_ref, total_ref):
    f32 = jnp.float32
    count, _, cols = parts_ref.shape
    tall = grad_ref.shape[0]
    for j in range(count):
        grad_ref[:, j * cols : (j + 1) * cols] = parts_ref[j, :tall].astype(f32)
    lines = jnp.sum(parts_ref[:, tall:].astype(f32), axis=0)
    total_ref[0] = jnp.sum(lines[:3, :1])


def unpack(parts, tall):
    count, _, cols = parts.shape
    return pl.pallas_call(
        unpack_kernel,
        out_shape=(
            jax.ShapeDtypeStruct((tall, count * cols), jnp.float32),
            jax.ShapeDtypeStruct((1,), jnp.float32),
        ),
        out_specs=(pl.BlockSpec(memory_space=pltpu.VMEM), pl.BlockSpec(memory_space=pltpu.SMEM)),
        compiler_params=pltpu.CompilerParams(vmem_limit_bytes=8 * 1024 * 1024),
    )(parts)


def on_device(hidden, head_weight, teacher_logits, target_ids, segment_ids, pair_order):
    f32, bf16 = jnp.float32, jnp.bfloat16
    n_vocab = lax.axis_size("vocab")
    n_dp = lax.axis_size("dp")
    rows, feats = hidden.shape
    width = head_weight.shape[1]
    pairs = n_vocab // 2
    core = lax.axis_index("vocab") % 2
    same_core = [[2 * j + c for j in range(pairs)] for c in range(2)]
    swap = [(i, i ^ 1) for i in range(n_vocab)]
    side = math.isqrt(pairs)
    index = lax.axis_index("vocab")
    place_x, place_y = index // (2 * side), index // 2 % side

    def around(i, along_x, distance):
        x, y, c = i // (2 * side), i // 2 % side, i % 2
        x, y = ((x + distance) % side, y) if along_x else (x, (y + distance) % side)
        return (x * side + y) * 2 + c

    around_x = [[(i, around(i, True, d)) for i in range(n_vocab)] for d in range(side)]
    around_y = [[(i, around(i, False, d)) for i in range(n_vocab)] for d in range(side)]
    weight_full = lax.all_gather(head_weight, "dp", axis=0, tiled=True)
    by_group = lax.all_gather(hidden.T, "dp")
    by_pair = to_all(by_group, "vocab", same_core).reshape(pairs, n_dp, feats, rows)
    own_t = relayout(by_pair)
    other_t = lax.ppermute(own_t, "vocab", swap)
    place = lax.axis_index("dp")

    def by_core(own, other, axis):
        return jnp.stack([jnp.where(core == 0, own, other), jnp.where(core == 0, other, own)], axis=axis)

    mine = lax.dynamic_slice_in_dim(own_t, place * rows, rows, 1).reshape(pairs, feats, rows)
    theirs = lax.dynamic_slice_in_dim(other_t, place * rows, rows, 1).reshape(pairs, feats, rows)
    rows_t = by_core(mine, theirs, 1).reshape(n_vocab * feats, rows)
    into_margin, into_weight = pair_signs(segment_ids[0], pair_order[0])
    tn = (((0,), (0,)), ((), ()))
    nt = (((1,), (1,)), ((), ()))
    student = lax.dot_general(rows_t, weight_full, tn, preferred_element_type=f32)
    target = (target_ids - index * width)[:, None]
    every = lax.all_to_all(local_stats(student, teacher_logits, target, n_vocab), "vocab", 0, 0, tiled=True)
    logit_grad, chunks, objective = make_grad(
        every, student, teacher_logits, target, into_margin, into_weight, n_dp
    )
    chunks = lax.all_to_all(chunks, "dp", 0, 0, tiled=True)
    term = lax.dot_general(weight_full, logit_grad, nt, preferred_element_type=f32).astype(bf16)
    term = term.reshape(side * side, 2, feats, rows)
    kept = lax.dynamic_index_in_dim(term, core, 1, keepdims=False)
    sent = lax.dynamic_index_in_dim(term, 1 - core, 1, keepdims=False)
    term = kept.astype(f32) + lax.ppermute(sent, "vocab", swap).astype(f32)
    term = ring_sum(term.reshape(side, side, feats, rows), place_x, around_x)
    chunks, term = lax.optimization_barrier((chunks, term))
    partial = head_partial(
        core.astype(jnp.int32).reshape(1),
        objective,
        own_t,
        other_t,
        chunks.reshape(n_dp * rows, width // n_dp),
        pairs,
        16,
    )
    partial, term = lax.optimization_barrier((partial, term))
    parts = lax.all_to_all(partial, "dp", 0, 0, tiled=True)
    hidden_grad = ring_sum(term, place_y, around_y).astype(bf16).T
    head_grad, total = unpack(parts, 2 * feats)
    loss_value = total[0] / (rows * n_dp)
    return (hidden_grad, head_grad, loss_value)


def solution(mesh):
    return jax.shard_map(
        on_device,
        mesh=mesh,
        in_specs=(
            P("dp", "vocab"),
            P("dp", "vocab"),
            P("dp", "vocab"),
            P("dp"),
            P("dp", None),
            P("dp", None),
        ),
        out_specs=(P("dp", "vocab"), P("dp", "vocab"), P()),
        check_vma=False,
    )
```
